32 devices in a mesh: rep: 2 (over core), row: 4 (over y, x), col: 4 (over z).
Axes of the slice: x: 2, y: 2, z: 4, core: 2. Of those that a mesh axis runs over, the one named last changes fastest.
Arguments:
- residual: bfloat16 [4096, 2048], P(('rep', 'row'), 'col'), may hold values from -6 to 6
- post_gain: float32 [2048], replicated, may hold values from 0.25 to 1.75
- w_gate: bfloat16 [2048, 6144], P('row', 'col'), may hold values from -0.125 to 0.125
- w_up: bfloat16 [2048, 6144], P('row', 'col'), may hold values from -0.125 to 0.125
- w_down: bfloat16 [6144, 2048], P('col', 'row'), may hold values from -0.078125 to 0.078125
- next_gain: float32 [2048], replicated, may hold values from 0.25 to 1.75
- w_qkv: bfloat16 [2048, 4096], P('row', 'col'), may hold values from -0.125 to 0.125
- q_gain: float32 [128], replicated, may hold values from 0.25 to 1.75
- k_gain: float32 [128], replicated, may hold values from 0.25 to 1.75
- source: int32 [4096], P(('rep', 'row')), may hold values from 0 to 4095, as said below
Outputs:
- moved_residual: bfloat16 [4096, 2048], P(('rep', 'row'), 'col')
- moved_qkv: bfloat16 [4096, 4096], P(('rep', 'row'), 'col')
The draws below stay inside these ranges and needn't reach their ends.
Inputs may be any that keep to these rules, and one draw needn't show every extreme that they name: source is a permutation of all rows. Rows are grouped in blocks of 512 (block b holds rows b * 512 to (b + 1) * 512 - 1, blocks of replica 0 first); output block b takes its rows from input block b or from the block of the same row index in the other replica, at most 128 of them from the other replica, and some block takes exactly 128. A block takes as many rows from the other replica as it gives to it.
All inputs are finite; a program needn't handle non-finite values.
Results may differ from the reference program's by a relative error of at most 0.0065.
Values may be sent and summed in bfloat16 or wider, within the bound.
No kernel may reach another device: no remote copies, remote signals or barrier semaphores. Data moves between devices by JAX's collectives and lax.ppermute only.
A program may use at most 64 MiB of HBM per device.

```python
import jax
import jax.numpy as jnp
from jax import lax

D = 2048
FF = 6144
HEADS = 16
KV_HEADS = 8
HD = 128
TPD = 512
QKV = 4096
MOVE = 128
TOKENS = 4096
N_ROW = 4


def draw_source(key, part):
    count_key, pick_key, rank_key, slot_key = jax.random.split(key, 4)
    moving_count = jax.random.randint(count_key, (N_ROW,), 0, MOVE + 1)
    forced_pair = jax.random.randint(pick_key, (), 0, N_ROW)
    moving_count = jnp.where(jnp.arange(N_ROW) == forced_pair, MOVE, moving_count).astype(jnp.int32)
    rank_keys = jax.random.split(rank_key, 2 * N_ROW)
    slot_keys = jax.random.split(slot_key, 2 * N_ROW)
    order_rank = jax.vmap(lambda subkey: jax.random.permutation(subkey, TPD))(rank_keys).astype(jnp.int32).reshape(2, N_ROW, TPD)
    slot_table = jax.vmap(lambda subkey: jax.random.permutation(subkey, TPD))(slot_keys).astype(jnp.int32).reshape(2, N_ROW, TPD)
    limit = moving_count[None, :, None]
    going = order_rank < limit
    replica = jnp.broadcast_to(jnp.arange(2, dtype=jnp.int32)[:, None, None], (2, N_ROW, TPD))
    row_index = jnp.broadcast_to(jnp.arange(N_ROW, dtype=jnp.int32)[None, :, None], (2, N_ROW, TPD))
    target = jnp.where(going, 1 - replica, replica)
    place = jnp.where(going, TPD - limit + order_rank, order_rank - limit)
    slot_value = slot_table[target, row_index, place]
    destination = ((target * N_ROW + row_index) * TPD + slot_value).reshape(-1)
    return jnp.zeros((TOKENS,), jnp.int32).at[destination].set(jnp.arange(TOKENS, dtype=jnp.int32))


def block_levels(own_key, extent, pieces, smallest, top_value):
    level = 1.0
    for position, parts in pieces:
        heights = jax.random.uniform(jax.random.fold_in(jax.random.fold_in(own_key, 6), position), (parts,), jnp.float32, smallest / len(pieces), top_value / len(pieces))
        level = level * jnp.repeat(jnp.exp(heights), extent[position] // parts).reshape((-1,) + (1,) * (len(extent) - 1 - position))
    return level


def gaussian(rng, shape, scale, most, pieces=(), kind=jnp.bfloat16):
    values = scale * jax.random.normal(rng, shape, jnp.float32)
    if pieces:
        values = values * block_levels(rng, shape, pieces, -0.22, 0.18)
    return jnp.clip(values, -most, most).astype(kind)


def setup_inputs(seed: int = 0) -> dict:
    keys = jax.random.split(jax.random.key(seed), 11)
    return {
        "residual": gaussian(keys[0], (TOKENS, D), 1.0, 6.0, ((0, 8), (1, 4))),
        "post_gain": jnp.clip(1.0 + 0.15 * jax.random.normal(keys[1], (D,), jnp.float32), 0.25, 1.75),
        "w_gate": gaussian(keys[2], (D, FF), D ** -0.5, 0.125, ((0, 4), (1, 4))),
        "w_up": gaussian(keys[3], (D, FF), D ** -0.5, 0.125, ((0, 4), (1, 4))),
        "w_down": gaussian(keys[4], (FF, D), FF ** -0.5, 0.078125, ((0, 4), (1, 4))),
        "next_gain": jnp.clip(1.0 + 0.15 * jax.random.normal(keys[5], (D,), jnp.float32), 0.25, 1.75),
        "w_qkv": gaussian(keys[6], (D, QKV), D ** -0.5, 0.125, ((0, 4), (1, 4))),
        "q_gain": jnp.clip(1.0 + 0.15 * jax.random.normal(keys[7], (HD,), jnp.float32), 0.25, 1.75),
        "k_gain": jnp.clip(1.0 + 0.15 * jax.random.normal(keys[8], (HD,), jnp.float32), 0.25, 1.75),
        "source": draw_source(jax.random.fold_in(keys[10], 71), 0),
    }


epsilon = 1e-06

def normalize(values, gain):
    scale = jax.lax.rsqrt(lax.optimization_barrier(jnp.mean(values * values, axis=-1, keepdims=True)) + epsilon)
    return values * scale * gain

def reference(residual, post_gain, w_gate, w_up, w_down, next_gain, w_qkv, q_gain, k_gain, source):
    stream = residual.astype(jnp.float32)
    normed = normalize(stream, post_gain).astype(jnp.bfloat16)
    gate_proj = jnp.dot(normed, w_gate, preferred_element_type=jnp.float32)
    up_proj = jnp.dot(normed, w_up, preferred_element_type=jnp.float32)
    hidden = (jax.nn.silu(gate_proj) * up_proj).astype(jnp.bfloat16)
    mlp_out = jnp.dot(hidden, w_down, preferred_element_type=jnp.float32)
    new_residual = (stream + mlp_out).astype(jnp.bfloat16)
    next_normed = normalize(new_residual.astype(jnp.float32), next_gain).astype(jnp.bfloat16)
    projected = jnp.dot(next_normed, w_qkv, preferred_element_type=jnp.float32)
    row_count = projected.shape[0]
    query_part = projected[:, :HEADS * HD].reshape(row_count, HEADS, HD)
    key_part = projected[:, HEADS * HD:(HEADS + KV_HEADS) * HD].reshape(row_count, KV_HEADS, HD)
    value_part = projected[:, (HEADS + KV_HEADS) * HD:]
    query_part = normalize(query_part, q_gain).reshape(row_count, HEADS * HD)
    key_part = normalize(key_part, k_gain).reshape(row_count, KV_HEADS * HD)
    qkv = jnp.concatenate([query_part, key_part, value_part], axis=1).astype(jnp.bfloat16)
    moved_residual = jnp.take(new_residual, source, axis=0)
    moved_qkv = jnp.take(qkv, source, axis=0)
    return (moved_residual, moved_qkv)
```

```python
import jax
import jax.numpy as jnp
from jax import lax
from jax.sharding import PartitionSpec as P

HEADS = 16
KV_HEADS = 8
HD = 128
epsilon = 1e-06
bf16, f32 = jnp.bfloat16, jnp.float32


def swap_cores(x):
    return lax.ppermute(x, "rep", [(0, 1), (1, 0)])


def bits_of(n):
    return n.bit_length() - 1


def row_step(x, step):
    rows = lax.axis_size("row")
    last = bits_of(rows) - 1
    pairs = []
    for core in range(2):
        mask = 1 << (step if core == 0 else last - step)
        pairs += [(core * rows + i, core * rows + (i ^ mask)) for i in range(rows)]
    return lax.ppermute(x, ("rep", "row"), pairs)


def mirrored(mask, bits):
    return sum(1 << (bits - 1 - b) for b in range(bits) if mask >> b & 1)


def gather_halves(half):
    rows = lax.axis_size("row")
    bits = bits_of(rows)
    held = {0: half}
    for step in range(bits):
        for mask in list(held):
            held[mask | 1 << step] = row_step(held[mask], step)
    mine = held
    swapped = {mask: swap_cores(piece) for mask, piece in held.items() if mask}
    return mine, swapped


def placed_rows(own, mine, swapped, core):
    rows = lax.axis_size("row")
    bits = bits_of(rows)
    out = [own]
    for mask in range(1, rows):
        other = mirrored(mask, bits)
        first = jnp.where(core == 0, mine[mask], swapped[mask])
        second = jnp.where(core == 0, swapped[other], mine[other])
        out += [first, second]
    return jnp.concatenate(out, axis=0)


def gather_line(x, cols):
    up = [(i, i + 1) for i in range(cols - 1)]
    down = [(i + 1, i) for i in range(cols - 1)]
    below, above = [], []
    a = d = x
    for _ in range(cols - 1):
        a = lax.ppermute(a, "col", up)
        d = lax.ppermute(d, "col", down)
        below.append(a)
        above.append(d)
    return below[::-1] + [x] + above


def sum_line(own, cols):
    total = own
    carry = own.astype(bf16)
    for hop in range(cols - 1):
        got = lax.ppermute(carry, "col", [(hop, hop + 1), (cols - 1 - hop, cols - 2 - hop)])
        got = got.astype(f32)
        total = total + got
        carry = (own + got).astype(bf16)
    return total


def per_device(residual, post_gain, w_gate, w_up, w_down, next_gain, w_qkv, q_gain, k_gain, source):
    rows, cols = lax.axis_size("row"), lax.axis_size("col")
    me, core, col = lax.axis_index("row"), lax.axis_index("rep"), lax.axis_index("col")
    tok, width = residual.shape
    d_model = width * cols
    block = d_model // rows
    ff = w_gate.shape[1]

    my_block = core * rows + me
    from_peer = source // tok != my_block
    picked = source % tok + tok * from_peer.astype(jnp.int32)
    onehot = (picked[:, None] == jnp.arange(2 * tok, dtype=jnp.int32)[None, :]).astype(bf16)
    both = jnp.concatenate([residual, swap_cores(residual)], axis=0)
    placed = jnp.dot(onehot, both, preferred_element_type=f32).astype(bf16)

    line = jnp.concatenate(gather_line(placed, cols), axis=1)

    def rel(mask):
        at = (cols - 1 + (me ^ mask) - col) * block
        return lax.dynamic_slice_in_dim(line, at, block, 1)

    stream = jnp.concatenate([rel(m) for m in range(rows)], axis=1)

    def rel_gain(gain):
        g = gain.reshape(rows, block)
        return jnp.concatenate([lax.dynamic_index_in_dim(g, me ^ m, 0, False) for m in range(rows)])

    post_rel, next_rel = rel_gain(post_gain), rel_gain(next_gain)

    wide = stream.astype(f32)
    scale = lax.rsqrt(jnp.mean(wide * wide, axis=-1, keepdims=True) + epsilon)
    normed = (wide * scale * post_rel).astype(bf16)

    parts = 2 if ff % 512 == 0 else 1
    step = ff // parts
    half = block // 2
    hidden = []
    for n in range(parts):
        own = jnp.concatenate([w_gate[:, n * step:(n + 1) * step], w_up[:, n * step:(n + 1) * step]], axis=1)
        mine, swapped = gather_halves(lax.dynamic_slice_in_dim(own, core * half, half, 0))
        full = placed_rows(own, mine, swapped, core)
        both_proj = jnp.dot(normed, full, preferred_element_type=f32)
        hidden.append((jax.nn.silu(both_proj[:, :step]) * both_proj[:, step:]).astype(bf16))
    hidden = jnp.concatenate(hidden, axis=1) if parts > 1 else hidden[0]

    chunks = max(1, min(4, block // 128))
    w = block // chunks
    groups = [[0], [1], [2, 3]] if chunks == 4 else [[c] for c in range(chunks)]
    new_chunks = []
    ff_half = ff // 2
    for group in groups:
        own = w_down[:, group[0] * w:(group[-1] + 1) * w]
        mine, swapped = gather_halves(lax.dynamic_slice_in_dim(own, core * ff_half, ff_half, 0))
        bits = bits_of(rows)
        cols_full = [own]
        for mask in range(1, rows):
            other = mirrored(mask, bits)
            cols_full.append(jnp.concatenate([
                jnp.where(core == 0, mine[mask], swapped[mask]),
                jnp.where(core == 0, swapped[other], mine[other])], axis=0))
        for k, c in enumerate(group):
            rhs = jnp.concatenate([b[:, k * w:(k + 1) * w] for b in cols_full], axis=1)
            part = jnp.dot(hidden, rhs, preferred_element_type=f32)
            total = sum_line(part, cols)
            here = jnp.concatenate([stream[:, m * block + c * w:m * block + (c + 1) * w] for m in range(rows)], axis=1)
            new_chunks.append((here.astype(f32) + total).astype(bf16))

    mine, swapped = gather_halves(lax.dynamic_slice_in_dim(w_qkv, core * half, half, 0))
    full = placed_rows(w_qkv, mine, swapped, core)
    proj_width = w_qkv.shape[1]
    acc = jnp.zeros((tok, proj_width), f32)
    squares = jnp.zeros((tok, 1), f32)
    full_blocks = full.reshape(rows, chunks, w, proj_width)
    gain_blocks = next_rel.reshape(rows, chunks, w)
    for c in range(chunks):
        v = new_chunks[c].astype(f32)
        squares = squares + jnp.sum(v * v, axis=-1, keepdims=True)
        lhs = (v * gain_blocks[:, c].reshape(-1)).astype(bf16)
        acc = acc + jnp.dot(lhs, full_blocks[:, c].reshape(rows * w, proj_width), preferred_element_type=f32)
    projected = acc * lax.rsqrt(squares / d_model + epsilon)

    head_count = proj_width // HD
    per_head = projected.reshape(tok, head_count, HD)
    head_number = col * head_count + jnp.arange(head_count, dtype=jnp.int32)
    is_query = head_number < HEADS
    keep_norm = (head_number < HEADS + KV_HEADS)[None, :, None]
    head_gain = jnp.where(is_query[:, None], q_gain[None, :], k_gain[None, :])
    head_scale = lax.rsqrt(jnp.mean(per_head * per_head, axis=-1, keepdims=True) + epsilon)
    moved_qkv = jnp.where(keep_norm, per_head * head_scale * head_gain, per_head)
    moved_qkv = moved_qkv.reshape(tok, proj_width).astype(bf16)

    at = (me ^ col) * w
    moved_residual = jnp.concatenate(
        [lax.dynamic_slice_in_dim(chunk, at, w, 1) for chunk in new_chunks], axis=1)
    return (moved_residual, moved_qkv)


def solution(mesh):
    return jax.shard_map(
        per_device,
        mesh=mesh,
        in_specs=(
            P(("rep", "row"), "col"),
            P(),
            P("row", "col"),
            P("row", "col"),
            P("col", "row"),
            P(),
            P("row", "col"),
            P(),
            P(),
            P(("rep", "row")),
        ),
        out_specs=(P(("rep", "row"), "col"), P(("rep", "row"), "col")),
        check_vma=False,
    )
```

```python
import functools

import jax
import jax.numpy as jnp
from jax import lax
from jax.experimental import pallas as pl
from jax.experimental.pallas import tpu as pltpu
from jax.sharding import PartitionSpec as P

HEADS = 16
KV_HEADS = 8
HD = 128
epsilon = 1e-06
bf16, f32 = jnp.bfloat16, jnp.float32
VMEM_LIMIT = 48 * 1024 * 1024


def swap_cores(x):
    return lax.ppermute(x, "rep", [(0, 1), (1, 0)])


def bits_of(n):
    return n.bit_length() - 1


def after(x, *done):
    return lax.optimization_barrier((x,) + done)[0] if done else x


def mirrored(mask, bits):
    return sum(1 << (bits - 1 - b) for b in range(bits) if mask >> b & 1)


def row_step(x, step):
    rows = lax.axis_size("row")
    last = bits_of(rows) - 1
    pairs = []
    for core in range(2):
        mask = 1 << (step if core == 0 else last - step)
        pairs += [(core * rows + i, core * rows + (i ^ mask)) for i in range(rows)]
    return lax.ppermute(x, ("rep", "row"), pairs)


def transfers(rows):
    order = [(1 << step, 0, step) for step in range(bits_of(rows))]
    for step in range(bits_of(rows)):
        order += [(held | 1 << step, held, step) for held in range(1, 1 << step)]
    return order


def tile_of(n):
    return next(t for t in (256, 128, n) if n % t == 0)


def project_kernel(n, has_acc, d_model, at_ref, *refs):
    lhs, ws, rest = refs[:n], refs[n:2 * n], refs[2 * n:]
    out_ref = rest[-1]
    x = jnp.concatenate([r[...] for r in lhs], axis=1)
    w = jnp.concatenate([r[...] for r in ws], axis=0)
    v = jnp.dot(x, w, preferred_element_type=f32)
    if has_acc:
        v = v + rest[0][...]
    if d_model is None:
        out_ref[...] = v
        return
    squares_ref, q_gain_ref, k_gain_ref = rest[-4:-1]
    v = v * lax.rsqrt(squares_ref[...] / d_model + epsilon)
    heads = v.shape[1] // HD
    for h in range(heads):
        number = at_ref[0] + pl.program_id(0) * heads + h
        one = v[:, h * HD:(h + 1) * HD]
        gain = jnp.where(number < HEADS, q_gain_ref[...], k_gain_ref[...])
        normed = one * lax.rsqrt(jnp.mean(one * one, axis=-1, keepdims=True) + epsilon) * gain
        out_ref[:, h * HD:(h + 1) * HD] = jnp.where(number < HEADS + KV_HEADS, normed, one).astype(bf16)


def project(acc, terms, first_head=None, final=None, d_model=None):
    tok, depth = terms[0][0].shape
    width = terms[0][1].shape[1]
    tn = tile_of(width)
    n = len(terms)
    tile = pl.BlockSpec((tok, tn), lambda i: (0, i))
    in_specs = [pl.BlockSpec(memory_space=pltpu.SMEM)]
    in_specs += [pl.BlockSpec((tok, depth), lambda i: (0, 0))] * n
    in_specs += [pl.BlockSpec((depth, tn), functools.partial(lambda r, i: (r, i), r)) for _, _, r in terms]
    args = [t[0] for t in terms] + [t[1] for t in terms]
    if acc is not None:
        in_specs, args = in_specs + [tile], args + [acc]
    if final is not None:
        in_specs += [pl.BlockSpec((tok, 1), lambda i: (0, 0))] + [pl.BlockSpec((1, HD), lambda i: (0, 0))] * 2
        args += list(final)
    first_head = jnp.zeros((1,), jnp.int32) if first_head is None else first_head.astype(jnp.int32).reshape(1)
    return pl.pallas_call(
        functools.partial(project_kernel, n, acc is not None, d_model),
        grid=(width // tn,),
        in_specs=in_specs,
        out_specs=tile,
        out_shape=jax.ShapeDtypeStruct((tok, width), f32 if final is None else bf16),
        compiler_params=pltpu.CompilerParams(vmem_limit_bytes=VMEM_LIMIT),
        cost_estimate=pl.CostEstimate(flops=2 * n * tok * depth * width,
                                      bytes_accessed=2 * n * depth * (width + tok) + 8 * tok * width, transcendentals=0),
    )(first_head, *args)


def per_device(residual, post_gain, w_gate, w_up, w_down, next_gain, w_qkv, q_gain, k_gain, source):
    rows, cols = lax.axis_size("row"), lax.axis_size("col")
    me, core, col = lax.axis_index("row"), lax.axis_index("rep"), lax.axis_index("col")
    tok, width = residual.shape
    d_model = width * cols
    block = d_model // rows
    half = block // 2
    bits = bits_of(rows)
    order = transfers(rows)
    direct = [o[0] for o in order if o[1] == 0]
    relayed = [o[0] for o in order if o[1] != 0]
    frames = [0] + direct + relayed

    def row_of(mask):
        return me ^ jnp.where(core == 0, mask, mirrored(mask, bits))

    barrier = lax.optimization_barrier
    even = [(i, i ^ 1) for i in range(cols)]
    odd = [(i, (i - 1 ^ 1) + 1) for i in range(1, cols - 1)]
    ff = w_gate.shape[1]
    ff_half = ff // 2
    last_mask = frames[-1]

    own = {"gate": w_gate, "up": w_up}
    gu = {(n, 0): lax.dynamic_slice_in_dim(w, core * half, half, 0) for n, w in own.items()}

    my_block = core * rows + me
    from_peer = after(source, gu["gate", 0]) // tok != my_block
    picked = source % tok + tok * from_peer.astype(jnp.int32)
    onehot = (picked[:, None] == jnp.arange(2 * tok, dtype=jnp.int32)[None, :]).astype(bf16)
    both = jnp.concatenate([residual, swap_cores(residual)], axis=0)
    placed = jnp.dot(onehot, both, preferred_element_type=f32).astype(bf16)

    by_even, by_odd = {0: placed}, {0: placed}
    left_over = cols - 1
    step = 0

    def line_step():
        nonlocal step
        if step < left_over:
            step += 1
            by_even[step] = lax.ppermute(by_odd[step - 1], "col", even)
            if step < left_over:
                by_odd[step] = lax.ppermute(by_even[step - 1], "col", odd)

    for n in own:
        for m in direct:
            gu[n, m] = row_step(gu[n, 0], bits_of(m))
        line_step()
        keys = [(n, m) for m in direct]
        ready = barrier(tuple(gu[k] for k in keys) + (by_even[step], by_odd[step], gu["up", 0]))
        for key, value in zip(keys, ready):
            gu[key] = value
        by_even[step], by_odd[step], gu["up", 0] = ready[len(keys):]
    for n in own:
        for mask, held, bit in order:
            if held:
                gu[n, mask] = row_step(gu[n, held], bit)
    while step < left_over:
        line_step()
    gu_other = {key: swap_cores(gu[key]) for key in gu if key[1]}

    arrived = [placed] + [by_even[t] for t in range(1, cols)] + [by_odd[t] for t in range(1, cols - 1)]
    place = [[0 if j == c else (abs(j - c) if (c % 2 == 1) == (j < c) else cols - 1 + abs(j - c))
              for j in range(cols)] for c in range(cols)]
    where_is = jnp.asarray(place, jnp.int32)[col]
    line = jnp.stack(arrived)
    blocks = {m: lax.dynamic_index_in_dim(line, where_is[row_of(m)], 0, False) for m in frames}

    squares = sum(jnp.sum(jnp.square(blocks[m].astype(f32)), axis=-1, keepdims=True) for m in frames)
    scale = lax.rsqrt(squares / d_model + epsilon)
    gains = post_gain.reshape(rows, block)

    def turned_halves(x):
        width = x.shape[1] // 2
        low, high = x[:, :width], x[:, width:]
        return jnp.concatenate([jnp.where(core == 0, low, high), jnp.where(core == 0, high, low)], axis=1)

    def normed(m):
        out = (blocks[m].astype(f32) * scale * lax.dynamic_index_in_dim(gains, row_of(m), 0, False)).astype(bf16)
        return out if m == 0 else turned_halves(out)

    def dot(x, w):
        return jnp.dot(x, w, preferred_element_type=f32)

    early, late = [0] + direct, relayed
    columns = [jnp.concatenate([normed(m) for m in ms], axis=1) for ms in (early, late)]

    def weights(n, masks):
        pieces = []
        for m in masks:
            pieces += [gu[n, m], gu_other[n, mirrored(m, bits)]] if m else [own[n]]
        return jnp.concatenate(pieces, axis=0)

    w_down_half = lax.dynamic_slice_in_dim(w_down, core * ff_half, ff_half, 0)
    w_qkv_half = lax.dynamic_slice_in_dim(w_qkv, core * half, half, 0)
    dn, dn_other, partial = {0: w_down_half}, {}, {}
    wq, wq_other = {0: w_qkv_half}, {}
    gate_early, up_early = (dot(columns[0], weights(n, early)) for n in own)
    keys = [(n, m) for n in own for m in relayed]
    ready = barrier(tuple(gu[k] for k in keys) + (gate_early, up_early, w_down_half))
    for key, value in zip(keys, ready):
        gu[key] = value
        gu_other[key] = swap_cores(value)
    gate_early, up_early, dn[0] = ready[len(keys):]
    for m in direct:
        dn[m] = row_step(dn[0], bits_of(m))
    gate = gate_early + dot(columns[1], weights("gate", late))
    up_proj = up_early + dot(columns[1], weights("up", late))
    hidden = (gate / (1 + jnp.exp(-gate)) * up_proj).astype(bf16)
    partial[0] = dot(hidden, w_down)
    turned = turned_halves(hidden)
    first_sent = partial[0].astype(bf16)

    def down_product(m):
        return dot(turned, jnp.concatenate([dn[m], dn_other[mirrored(m, bits)]], axis=0))

    from_low = col % 2 == 1
    place_even = jnp.where(from_low, cols - 1 - col, col)
    place_odd = jnp.where(from_low, col, cols - 1 - col)
    by_even, by_odd = {}, {}

    def placed_at(t, place, places):
        value = None
        for c in places:
            if 0 <= t - c < rows:
                value = partial[t - c] if value is None else jnp.where(place == c, partial[t - c], value)
        return value

    def bases(t):
        return [placed_at(t, place_even, range(0, cols - 1, 2)), placed_at(t, place_odd, range(1, cols - 1, 2))]

    def terms(k):
        found = {}
        for c in range(cols):
            if c > 0:
                found.setdefault((c % 2, k + c - 1), []).append(c)
            if c < cols - 1:
                found.setdefault(((c + 1) % 2, k + cols - 2 - c), []).append(c)
        return found

    def summed(k):
        total = partial[k]
        for (is_even, t), where in terms(k).items():
            came = (by_even if is_even else by_odd)[t].astype(f32)
            counts = functools.reduce(jnp.logical_or, [col == c for c in where])
            total = total + jnp.where(counts, came, 0)
        return total

    next_gains = next_gain.reshape(rows, 1, block)
    squares, fresh, scaled = {}, {}, {}

    def finish(k):
        m = frames[k]
        fresh[k] = (blocks[m].astype(f32) + summed(k)).astype(bf16)
        v = fresh[k].astype(f32)
        squares[k] = jnp.sum(v * v, axis=-1, keepdims=True)
        out = (v * lax.dynamic_index_in_dim(next_gains, row_of(m), 0, False)).astype(bf16)
        scaled[k] = out if m == 0 else turned_halves(out)

    def terms_of(k):
        m = frames[k]
        low, high = scaled[k][:, :half], scaled[k][:, half:]
        if m == 0:
            return [(low, w_qkv, 0), (high, w_qkv, 1)]
        return [(low, wq[m], 0), (high, wq_other[mirrored(m, bits)], 0)]

    place_of = {m: k for k, m in enumerate(frames)}
    steps = rows + cols - 2
    ready = barrier(tuple(dn[m] for m in direct) + (first_sent,))
    for m, value in zip(direct, ready):
        dn[m] = value
        dn_other[m] = swap_cores(value)
    first_sent = ready[-1]
    for mask, held, bit in order:
        if held:
            dn[mask] = row_step(dn[held], bit)
    acc, last_step = None, ()

    def tie(store, masks, values):
        for m, value in zip(masks, values):
            store[m] = value

    for t in range(steps):
        base = bases(t)
        sends = []
        for i, came in enumerate((by_odd.get(t - 1), by_even.get(t - 1))):
            if base[i] is not None:
                send = base[i] if came is None else base[i] + came.astype(f32)
                sends.append((i, first_sent if t == 0 else send.astype(bf16)))
        held_now = {0: [(dn_other, direct)], 1: [(dn, relayed), (partial, [place_of[m] for m in direct])],
                    2: [(dn_other, relayed), (wq, direct)],
                    3: [(wq, relayed), (wq_other, direct), (partial, [place_of[m] for m in relayed])],
                    4: [(wq_other, relayed)]}.get(t, [])
        flat = [store[m] for store, masks in held_now for m in masks]
        extra = [acc] if t == steps - 1 else []
        ready = barrier(tuple(v for _, v in sends) + tuple(flat) + tuple(last_step) + tuple(extra))
        for (i, _), send in zip(sends, ready):
            (by_even, by_odd)[i][t] = lax.ppermute(send, "col", (even, odd)[i])
        at = len(sends)
        for store, masks in held_now:
            tie(store, masks, ready[at:at + len(masks)])
            at += len(masks)
        if extra:
            acc = ready[-1]
        last_step = [(by_even, by_odd)[i][t] for i, _ in sends]
        if t == 0:
            for m in direct:
                partial[place_of[m]] = down_product(m)
        elif t == 1:
            for m in relayed:
                dn_other[m] = swap_cores(dn[m])
            for m in direct:
                wq[m] = row_step(wq[0], bits_of(m))
        elif t == 2:
            for m in relayed:
                partial[place_of[m]] = down_product(m)
            for m in direct:
                wq_other[m] = swap_cores(wq[m])
            for mask, held, bit in order:
                if held:
                    wq[mask] = row_step(wq[held], bit)
        elif t == 3:
            for m in relayed:
                wq_other[m] = swap_cores(wq[m])
        k = t - (cols - 2)
        if k >= 0:
            finish(k)
        if k == rows - 3:
            acc = project(None, [x for j in range(rows - 2) for x in terms_of(j)])
    acc = project(acc, terms_of(rows - 2))

    moved_residual = fresh[0]
    for k in range(1, rows):
        moved_residual = jnp.where(row_of(frames[k]) == col, fresh[k], moved_residual)
    moved_qkv = project(acc, terms_of(rows - 1), (w_qkv.shape[1] // HD) * col,
                        (sum(squares.values()), q_gain.reshape(1, HD), k_gain.reshape(1, HD)), d_model)
    return (moved_residual, moved_qkv)


def solution(mesh):
    return jax.shard_map(
        per_device,
        mesh=mesh,
        in_specs=(
            P(("rep", "row"), "col"),
            P(),
            P("row", "col"),
            P("row", "col"),
            P("col", "row"),
            P(),
            P("row", "col"),
            P(),
            P(),
            P(("rep", "row")),
        ),
        out_specs=(P(("rep", "row"), "col"), P(("rep", "row"), "col")),
        check_vma=False,
    )
```

```python
import functools

import jax
import jax.numpy as jnp
from jax import lax
from jax.experimental import pallas as pl
from jax.experimental.pallas import tpu as pltpu
from jax.sharding import PartitionSpec as P

HEADS = 16
KV_HEADS = 8
HD = 128
epsilon = 1e-06
bf16, f32 = jnp.bfloat16, jnp.float32
VMEM_LIMIT = 48 * 1024 * 1024


def swap_cores(x):
    return lax.ppermute(x, "rep", [(0, 1), (1, 0)])


def bits_of(n):
    return n.bit_length() - 1


def after(x, *done):
    return lax.optimization_barrier((x,) + done)[0] if done else x


def mirrored(mask, bits):
    return sum(1 << (bits - 1 - b) for b in range(bits) if mask >> b & 1)


def row_step(x, step):
    rows = lax.axis_size("row")
    last = bits_of(rows) - 1
    pairs = []
    for core in range(2):
        mask = 1 << (step if core == 0 else last - step)
        pairs += [(core * rows + i, core * rows + (i ^ mask)) for i in range(rows)]
    return lax.ppermute(x, ("rep", "row"), pairs)


def transfers(rows):
    order = [(1 << step, 0, step) for step in range(bits_of(rows))]
    for step in range(bits_of(rows)):
        order += [(held | 1 << step, held, step) for held in range(1, 1 << step)]
    return order


def tile_of(n):
    return next(t for t in (256, 128, n) if n % t == 0)


def project_kernel(n, has_acc, d_model, at_ref, *refs):
    lhs, ws, rest = refs[:n], refs[n:2 * n], refs[2 * n:]
    x = jnp.concatenate([r[...] for r in lhs], axis=1)
    w = jnp.concatenate([r[...] for r in ws], axis=0)
    v = jnp.dot(x, w, preferred_element_type=f32)
    if has_acc:
        v = v + rest[0][...]
    if d_model is None:
        rest[-1][...] = v
        return
    squares_ref, q_gain_ref, k_gain_ref, fresh_ref, other_ref, out_ref, moved_ref = rest[-7:]
    moved_ref[...] = jnp.where(at_ref[1] == 1, fresh_ref[...], other_ref[...])
    v = v * lax.rsqrt(squares_ref[...] / d_model + epsilon)
    heads = v.shape[1] // HD
    for h in range(heads):
        number = at_ref[0] + pl.program_id(0) * heads + h
        one = v[:, h * HD:(h + 1) * HD]
        gain = jnp.where(number < HEADS, q_gain_ref[...], k_gain_ref[...])
        normed = one * lax.rsqrt(jnp.mean(one * one, axis=-1, keepdims=True) + epsilon) * gain
        out_ref[:, h * HD:(h + 1) * HD] = jnp.where(number < HEADS + KV_HEADS, normed, one).astype(bf16)


def project(acc, terms, scalars, final=None, d_model=None):
    tok, depth = terms[0][0].shape
    width = terms[0][1].shape[1]
    tn = tile_of(width)
    n = len(terms)
    tile = pl.BlockSpec((tok, tn), lambda i: (0, i))
    in_specs = [pl.BlockSpec(memory_space=pltpu.SMEM)]
    in_specs += [pl.BlockSpec((tok, depth), lambda i: (0, 0))] * n
    in_specs += [pl.BlockSpec((depth, tn), functools.partial(lambda r, i: (r, i), r)) for _, _, r in terms]
    args = [t[0] for t in terms] + [t[1] for t in terms]
    if acc is not None:
        in_specs, args = in_specs + [tile], args + [acc]
    if final is not None:
        block = final[-1].shape[1]
        moved = pl.BlockSpec((tok, block // (width // tn)), lambda i: (0, i))
        in_specs += [pl.BlockSpec((tok, 1), lambda i: (0, 0))] + [pl.BlockSpec((1, HD), lambda i: (0, 0))] * 2
        in_specs += [moved] * 2
        args += list(final)
    out_specs, out_shape = tile, jax.ShapeDtypeStruct((tok, width), f32)
    if final is not None:
        out_specs = [tile, moved]
        out_shape = [jax.ShapeDtypeStruct((tok, width), bf16), jax.ShapeDtypeStruct((tok, block), bf16)]
    return pl.pallas_call(
        functools.partial(project_kernel, n, acc is not None, d_model),
        grid=(width // tn,),
        in_specs=in_specs,
        out_specs=out_specs,
        out_shape=out_shape,
        compiler_params=pltpu.CompilerParams(vmem_limit_bytes=VMEM_LIMIT),
        cost_estimate=pl.CostEstimate(flops=2 * n * tok * depth * width,
                                      bytes_accessed=2 * n * depth * (width + tok) + 8 * tok * width, transcendentals=0),
    )(scalars, *args)


def per_device(residual, post_gain, w_gate, w_up, w_down, next_gain, w_qkv, q_gain, k_gain, source):
    rows, cols = lax.axis_size("row"), lax.axis_size("col")
    me, core, col = lax.axis_index("row"), lax.axis_index("rep"), lax.axis_index("col")
    tok, width = residual.shape
    d_model = width * cols
    block = d_model // rows
    half = block // 2
    bits = bits_of(rows)
    order = transfers(rows)
    direct = [o[0] for o in order if o[1] == 0]
    relayed = [o[0] for o in order if o[1] != 0]
    frames = [0] + direct + relayed

    def row_of(mask):
        return me ^ jnp.where(core == 0, mask, mirrored(mask, bits))

    barrier = lax.optimization_barrier
    even = [(i, i ^ 1) for i in range(cols)]
    odd = [(i, (i - 1 ^ 1) + 1) for i in range(1, cols - 1)]
    ff = w_gate.shape[1]
    ff_half = ff // 2
    last_mask = frames[-1]

    own = {"gate": w_gate, "up": w_up}
    gu = {0: jnp.concatenate([lax.dynamic_slice_in_dim(w, core * half, half, 0) for w in own.values()], axis=0)}

    my_block = core * rows + me
    from_peer = after(source, gu[0]) // tok != my_block
    picked = source % tok + tok * from_peer.astype(jnp.int32)
    onehot = (picked[:, None] == jnp.arange(2 * tok, dtype=jnp.int32)[None, :]).astype(bf16)
    both = jnp.concatenate([residual, swap_cores(residual)], axis=0)
    placed = jnp.dot(onehot, both, preferred_element_type=f32).astype(bf16)

    by_even, by_odd = {0: placed}, {0: placed}
    left_over = cols - 1
    step = 0

    def line_step():
        nonlocal step
        if step < left_over:
            step += 1
            by_even[step] = lax.ppermute(by_odd[step - 1], "col", even)
            if step < left_over:
                by_odd[step] = lax.ppermute(by_even[step - 1], "col", odd)

    for m in direct:
        gu[m] = row_step(gu[0], bits_of(m))
    for _ in range(left_over - 1):
        line_step()
    ready = barrier(tuple(gu[m] for m in direct) + (by_even[step], by_odd[step]))
    for m, value in zip(direct, ready):
        gu[m] = value
    by_even[step], by_odd[step] = ready[len(direct):]
    for mask, held, bit in order:
        if held:
            gu[mask] = row_step(gu[held], bit)
    line_step()
    arrived = [placed] + [by_even[t] for t in range(1, cols)] + [by_odd[t] for t in range(1, cols - 1)]
    place = [[0 if j == c else (abs(j - c) if (c % 2 == 1) == (j < c) else cols - 1 + abs(j - c))
              for j in range(cols)] for c in range(cols)]
    where_is = jnp.asarray(place, jnp.int32)[col]
    line = jnp.stack(arrived)
    blocks = {m: lax.dynamic_index_in_dim(line, where_is[row_of(m)], 0, False) for m in frames}

    squares = sum(jnp.sum(jnp.square(blocks[m].astype(f32)), axis=-1, keepdims=True) for m in frames)
    scale = lax.rsqrt(squares / d_model + epsilon)
    gains = post_gain.reshape(rows, block)

    def turned_halves(x):
        width = x.shape[1] // 2
        low, high = x[:, :width], x[:, width:]
        return jnp.concatenate([jnp.where(core == 0, low, high), jnp.where(core == 0, high, low)], axis=1)

    def normed(m):
        out = (blocks[m].astype(f32) * scale * lax.dynamic_index_in_dim(gains, row_of(m), 0, False)).astype(bf16)
        return out if m == 0 else turned_halves(out)

    def dot(x, w):
        return jnp.dot(x, w, preferred_element_type=f32)

    early, late = [0] + direct, relayed
    columns = [jnp.concatenate([normed(m) for m in ms], axis=1) for ms in (early, late)]

    w_down_half = lax.dynamic_slice_in_dim(w_down, core * ff_half, ff_half, 0)
    ready = barrier(tuple(gu[m] for m in relayed) + tuple(columns) + (w_down_half,))
    for m, value in zip(relayed, ready):
        gu[m] = value
    columns, w_down_half = ready[len(relayed):-1], ready[-1]
    gu_other = {m: swap_cores(gu[m]) for m in frames[1:]}

    def weights(n, masks):
        pieces, at = [], half * (n == "up")
        for m in masks:
            pieces += [x[at:at + half] for x in (gu[m], gu_other[mirrored(m, bits)])] if m else [own[n]]
        return jnp.concatenate(pieces, axis=0)

    w_qkv_half = lax.dynamic_slice_in_dim(w_qkv, core * half, half, 0)
    dn, dn_other, partial = {0: w_down_half}, {}, {}
    wq, wq_other = {0: w_qkv_half}, {}
    for m in direct:
        dn[m] = row_step(dn[0], bits_of(m))
    gate_early, up_early = (dot(columns[0], weights(n, early)) for n in own)
    gate = gate_early + dot(columns[1], weights("gate", late))
    up_proj = up_early + dot(columns[1], weights("up", late))
    hidden = (gate / (1 + jnp.exp(-gate)) * up_proj).astype(bf16)
    partial[0] = dot(hidden, w_down).astype(bf16)
    turned = turned_halves(hidden)
    first_sent = partial[0]

    def down_product(m):
        return dot(turned, jnp.concatenate([dn[m], dn_other[mirrored(m, bits)]], axis=0)).astype(bf16)

    from_low = col % 2 == 1
    place_even = jnp.where(from_low, cols - 1 - col, col)
    place_odd = jnp.where(from_low, col, cols - 1 - col)
    by_even, by_odd = {}, {}

    def placed_at(t, place, places):
        value = None
        for c in places:
            if 0 <= t - c < rows:
                value = partial[t - c] if value is None else jnp.where(place == c, partial[t - c], value)
        return value

    def bases(t):
        return [placed_at(t, place_even, range(0, cols - 1, 2)), placed_at(t, place_odd, range(1, cols - 1, 2))]

    def terms(k):
        found = {}
        for c in range(cols):
            if c > 0:
                found.setdefault((c % 2, k + c - 1), []).append(c)
            if c < cols - 1:
                found.setdefault(((c + 1) % 2, k + cols - 2 - c), []).append(c)
        return found

    def summed(k):
        total = partial[k].astype(f32)
        for (is_even, t), where in terms(k).items():
            came = (by_even if is_even else by_odd)[t].astype(f32)
            counts = functools.reduce(jnp.logical_or, [col == c for c in where])
            total = total + jnp.where(counts, came, 0)
        return total

    next_gains = next_gain.reshape(rows, 1, block)
    squares, fresh, scaled = {}, {}, {}

    def finish(k):
        m = frames[k]
        fresh[k] = (blocks[m].astype(f32) + summed(k)).astype(bf16)
        v = fresh[k].astype(f32)
        squares[k] = jnp.sum(v * v, axis=-1, keepdims=True)
        out = (v * lax.dynamic_index_in_dim(next_gains, row_of(m), 0, False)).astype(bf16)
        scaled[k] = out if m == 0 else turned_halves(out)

    def terms_of(k):
        m = frames[k]
        low, high = scaled[k][:, :half], scaled[k][:, half:]
        if m == 0:
            return [(low, w_qkv, 0), (high, w_qkv, 1)]
        return [(low, wq[m], 0), (high, wq_other[mirrored(m, bits)], 0)]

    place_of = {m: k for k, m in enumerate(frames)}
    steps = rows + cols - 2
    ready = barrier(tuple(dn[m] for m in direct) + (first_sent,))
    for m, value in zip(direct, ready):
        dn[m] = value
        dn_other[m] = swap_cores(value)
    first_sent = ready[-1]
    for mask, held, bit in order:
        if held:
            dn[mask] = row_step(dn[held], bit)
    acc, last_step = None, ()
    scalars = jnp.stack([(w_qkv.shape[1] // HD) * col, row_of(frames[-1]) == col]).astype(jnp.int32)

    def tie(store, masks, values):
        for m, value in zip(masks, values):
            store[m] = value

    for t in range(steps):
        base = bases(t)
        sends = []
        for i, came in enumerate((by_odd.get(t - 1), by_even.get(t - 1))):
            if base[i] is not None:
                send = base[i] if came is None else base[i].astype(f32) + came.astype(f32)
                sends.append((i, first_sent if t == 0 else send.astype(bf16)))
        held_now = {1: [(dn, relayed), (partial, [place_of[m] for m in direct])], 2: [(dn_other, relayed), (wq, direct[:1])],
                    3: [(wq, direct[1:]), (wq_other, direct[:1]), (partial, [place_of[m] for m in relayed])],
                    4: [(wq, relayed), (wq_other, direct[1:])]}.get(t, [])
        done = t - cols
        if done >= 0:
            held_now = held_now + [(fresh, [done]), (scaled, [done])]
        flat = [store[m] for store, masks in held_now for m in masks]
        extra = [acc] if t == steps - 1 else []
        ready = barrier(tuple(v for _, v in sends) + tuple(flat) + tuple(last_step) + tuple(extra))
        for (i, _), send in zip(sends, ready):
            (by_even, by_odd)[i][t] = lax.ppermute(send, "col", (even, odd)[i])
        at = len(sends)
        for store, masks in held_now:
            tie(store, masks, ready[at:at + len(masks)])
            at += len(masks)
        if extra:
            acc = ready[-1]
        if t > 0:
            for (i, _), value in zip(sent_before, ready[at:]):
                (by_even, by_odd)[i][t - 1] = value
        sent_before = sends
        last_step = [(by_even, by_odd)[i][t] for i, _ in sends]
        if t == 0:
            for m in direct:
                partial[place_of[m]] = barrier(down_product(m))
        elif t == 1:
            for m in relayed:
                dn_other[m] = swap_cores(dn[m])
            for m in direct[:1]:
                wq[m] = row_step(wq[0], bits_of(m))
        elif t == 2:
            for m in direct[1:]:
                wq[m] = row_step(wq[0], bits_of(m))
            for m in direct[:1]:
                wq_other[m] = swap_cores(wq[m])
            for m in relayed:
                partial[place_of[m]] = barrier(down_product(m))
        elif t == 3:
            for m in direct[1:]:
                wq_other[m] = swap_cores(wq[m])
            for mask, held, bit in order:
                if held:
                    wq[mask] = row_step(wq[held], bit)
        elif t == 4:
            for m in relayed:
                wq_other[m] = swap_cores(wq[m])
        k = t - (cols - 1)
        if k >= 0:
            finish(k)
        if k == rows - 3:
            acc = project(None, [x for j in range(rows - 2) for x in terms_of(j)], scalars)
    acc = project(acc, terms_of(rows - 2), scalars)
    finish(rows - 1)

    kept = fresh[0]
    for k in range(1, rows - 1):
        kept = jnp.where(row_of(frames[k]) == col, fresh[k], kept)
    moved_qkv, moved_residual = project(
        acc, terms_of(rows - 1), scalars,
        (sum(squares.values()), q_gain.reshape(1, HD), k_gain.reshape(1, HD), fresh[rows - 1], kept), d_model)
    return (moved_residual, moved_qkv)


def solution(mesh):
    return jax.shard_map(
        per_device,
        mesh=mesh,
        in_specs=(
            P(("rep", "row"), "col"),
            P(),
            P("row", "col"),
            P("row", "col"),
            P("col", "row"),
            P(),
            P("row", "col"),
            P(),
            P(),
            P(("rep", "row")),
        ),
        out_specs=(P(("rep", "row"), "col"), P(("rep", "row"), "col")),
        check_vma=False,
    )
```

```python
import functools

import jax
import jax.numpy as jnp
from jax import lax
from jax.experimental import pallas as pl
from jax.experimental.pallas import tpu as pltpu
from jax.sharding import PartitionSpec as P

HEADS = 16
KV_HEADS = 8
HD = 128
epsilon = 1e-06
bf16, f32 = jnp.bfloat16, jnp.float32
VMEM_LIMIT = 48 * 1024 * 1024


def swap_cores(x):
    return lax.ppermute(x, "rep", [(0, 1), (1, 0)])


def bits_of(n):
    return n.bit_length() - 1


def after(x, *done):
    return lax.optimization_barrier((x,) + done)[0] if done else x


def mirrored(mask, bits):
    return sum(1 << (bits - 1 - b) for b in range(bits) if mask >> b & 1)


def row_step(x, step):
    rows = lax.axis_size("row")
    last = bits_of(rows) - 1
    pairs = []
    for core in range(2):
        mask = 1 << (step if core == 0 else last - step)
        pairs += [(core * rows + i, core * rows + (i ^ mask)) for i in range(rows)]
    return lax.ppermute(x, ("rep", "row"), pairs)


def transfers(rows):
    order = [(1 << step, 0, step) for step in range(bits_of(rows))]
    for step in range(bits_of(rows)):
        order += [(held | 1 << step, held, step) for held in range(1, 1 << step)]
    return order


def tile_of(n):
    return next(t for t in (512, 256, 128, n) if n % t == 0)


def halves_kernel(core_ref, top_ref, bottom_ref, out_ref):
    half = top_ref.shape[0]
    out_ref[:half] = top_ref[...]
    out_ref[half:] = bottom_ref[...]


def core_halves(core, top, bottom):
    half, width = top.shape[0] // 2, top.shape[1]
    tn = next(t for t in (512, 384, 128, width) if width % t == 0)
    piece = pl.BlockSpec((half, tn), lambda i, c: (c[0], i))
    return pl.pallas_call(
        halves_kernel,
        grid_spec=pltpu.PrefetchScalarGridSpec(
            num_scalar_prefetch=1, grid=(width // tn,), in_specs=[piece, piece],
            out_specs=pl.BlockSpec((2 * half, tn), lambda i, c: (0, i))),
        out_shape=jax.ShapeDtypeStruct((2 * half, width), bf16),
        compiler_params=pltpu.CompilerParams(vmem_limit_bytes=VMEM_LIMIT),
        cost_estimate=pl.CostEstimate(flops=0, bytes_accessed=8 * half * width, transcendentals=0),
    )(core, top, bottom)


def project_kernel(n, has_acc, d_model, at_ref, *refs):
    lhs, ws, rest = refs[:n], refs[n:2 * n], refs[2 * n:]
    x = jnp.concatenate([r[...] for r in lhs], axis=1)
    w = jnp.concatenate([r[...] for r in ws], axis=0)
    v = jnp.dot(x, w, preferred_element_type=f32)
    if has_acc:
        v = v + rest[0][...]
    if d_model is None:
        rest[-1][...] = v
        return
    squares_ref, q_gain_ref, k_gain_ref, fresh_ref, other_ref, out_ref, moved_ref = rest[-7:]
    moved_ref[...] = jnp.where(at_ref[1] == 1, fresh_ref[...], other_ref[...])
    v = v * lax.rsqrt(squares_ref[...] / d_model + epsilon)
    heads = v.shape[1] // HD
    for h in range(heads):
        number = at_ref[0] + pl.program_id(0) * heads + h
        one = v[:, h * HD:(h + 1) * HD]
        gain = jnp.where(number < HEADS, q_gain_ref[...], k_gain_ref[...])
        normed = one * lax.rsqrt(jnp.mean(one * one, axis=-1, keepdims=True) + epsilon) * gain
        out_ref[:, h * HD:(h + 1) * HD] = jnp.where(number < HEADS + KV_HEADS, normed, one).astype(bf16)


def project(acc, terms, scalars, final=None, d_model=None):
    tok, depth = terms[0][0].shape
    width = terms[0][1].shape[1]
    tn = tile_of(width)
    n = len(terms)
    tile = pl.BlockSpec((tok, tn), lambda i: (0, i))
    in_specs = [pl.BlockSpec(memory_space=pltpu.SMEM)]
    in_specs += [pl.BlockSpec((tok, depth), lambda i: (0, 0))] * n
    in_specs += [pl.BlockSpec((depth, tn), functools.partial(lambda r, i: (r, i), r)) for _, _, r in terms]
    args = [t[0] for t in terms] + [t[1] for t in terms]
    if acc is not None:
        in_specs, args = in_specs + [tile], args + [acc]
    if final is not None:
        block = final[-1].shape[1]
        moved = pl.BlockSpec((tok, block // (width // tn)), lambda i: (0, i))
        in_specs += [pl.BlockSpec((tok, 1), lambda i: (0, 0))] + [pl.BlockSpec((1, HD), lambda i: (0, 0))] * 2
        in_specs += [moved] * 2
        args += list(final)
    out_specs, out_shape = tile, jax.ShapeDtypeStruct((tok, width), f32)
    if final is not None:
        out_specs = [tile, moved]
        out_shape = [jax.ShapeDtypeStruct((tok, width), bf16), jax.ShapeDtypeStruct((tok, block), bf16)]
    return pl.pallas_call(
        functools.partial(project_kernel, n, acc is not None, d_model),
        grid=(width // tn,),
        in_specs=in_specs,
        out_specs=out_specs,
        out_shape=out_shape,
        compiler_params=pltpu.CompilerParams(vmem_limit_bytes=VMEM_LIMIT),
        cost_estimate=pl.CostEstimate(flops=2 * n * tok * depth * width,
                                      bytes_accessed=2 * n * depth * (width + tok) + 8 * tok * width, transcendentals=0),
    )(scalars, *args)


def per_device(residual, post_gain, w_gate, w_up, w_down, next_gain, w_qkv, q_gain, k_gain, source):
    rows, cols = lax.axis_size("row"), lax.axis_size("col")
    me, core, col = lax.axis_index("row"), lax.axis_index("rep"), lax.axis_index("col")
    tok, width = residual.shape
    d_model = width * cols
    block = d_model // rows
    half = block // 2
    bits = bits_of(rows)
    order = transfers(rows)
    direct = [o[0] for o in order if o[1] == 0]
    relayed = [o[0] for o in order if o[1] != 0]
    frames = [0] + direct + relayed

    def row_of(mask):
        return me ^ jnp.where(core == 0, mask, mirrored(mask, bits))

    barrier = lax.optimization_barrier
    even = [(i, i ^ 1) for i in range(cols)]
    odd = [(cols * r + i, cols * r + (i - 1 ^ 1) + 1) for r in range(2) for i in range(1, cols - 1)]
    odd += [(cols * r + i, cols * (1 - r) + i) for r in range(2) for i in (0, cols - 1)]
    line_axes = ("col", ("rep", "col"))
    at_end = (col == 0) | (col == cols - 1)
    ff = w_gate.shape[1]
    ff_half = ff // 2
    last_mask = frames[-1]

    own = {"gate": w_gate, "up": w_up}
    gu = {0: core_halves(core.astype(jnp.int32).reshape(1), w_gate, w_up)}

    my_block = core * rows + me
    from_peer = after(source, gu[0]) // tok != my_block
    picked = source % tok + tok * from_peer.astype(jnp.int32)
    onehot = (picked[:, None] == jnp.arange(2 * tok, dtype=jnp.int32)[None, :]).astype(bf16)
    both = jnp.concatenate([residual, swap_cores(residual)], axis=0)
    placed = jnp.dot(onehot, both, preferred_element_type=f32).astype(bf16)

    by_even, by_odd = {0: placed}, {0: placed}
    left_over = cols - 1
    step = 0

    def line_step():
        nonlocal step
        if step < left_over:
            step += 1
            by_even[step] = lax.ppermute(by_odd[step - 1], "col", even)
            if step < left_over:
                by_odd[step] = lax.ppermute(by_even[step - 1], line_axes[1], odd)

    for m in direct:
        gu[m] = row_step(gu[0], bits_of(m))
    for _ in range(left_over):
        line_step()
    before = max(left_over - 1, 0)
    ready = barrier(tuple(gu[m] for m in direct) + (by_even[before], by_odd[before]))
    for m, value in zip(direct, ready):
        gu[m] = value
    by_even[before], by_odd[before] = ready[len(direct):]
    for mask, held, bit in order:
        if held:
            gu[mask] = row_step(gu[held], bit)

    arrived = [placed] + [by_even[t] for t in range(1, cols)] + [by_odd[t] for t in range(1, cols - 1)]
    place = [[0 if j == c else (abs(j - c) if (c % 2 == 1) == (j < c) else cols - 1 + abs(j - c))
              for j in range(cols)] for c in range(cols)]
    where_is = jnp.asarray(place, jnp.int32)[col]
    line = jnp.stack(arrived)
    blocks = {m: lax.dynamic_index_in_dim(line, where_is[row_of(m)], 0, False) for m in frames}

    squares = sum(jnp.sum(jnp.square(blocks[m].astype(f32)), axis=-1, keepdims=True) for m in frames)
    scale = lax.rsqrt(squares / d_model + epsilon)
    gains = post_gain.reshape(rows, block)

    def turned_halves(x):
        width = x.shape[1] // 2
        low, high = x[:, :width], x[:, width:]
        return jnp.concatenate([jnp.where(core == 0, low, high), jnp.where(core == 0, high, low)], axis=1)

    def normed(m):
        out = (blocks[m].astype(f32) * scale * lax.dynamic_index_in_dim(gains, row_of(m), 0, False)).astype(bf16)
        return out if m == 0 else turned_halves(out)

    def dot(x, w):
        return jnp.dot(x, w, preferred_element_type=f32)

    early, late = [0] + direct, relayed
    columns = [jnp.concatenate([normed(m) for m in ms], axis=1) for ms in (early, late)]

    w_down_half = lax.dynamic_slice_in_dim(w_down, core * ff_half, ff_half, 0)
    ready = barrier(tuple(gu[m] for m in relayed) + tuple(columns) + (w_down_half,))
    for m, value in zip(relayed, ready):
        gu[m] = value
    columns, w_down_half = ready[len(relayed):-1], ready[-1]
    gu_other = {m: swap_cores(gu[m]) for m in frames[1:]}

    def weights(n, masks):
        pieces, at = [], half * (n == "up")
        for m in masks:
            pieces += [x[at:at + half] for x in (gu[m], gu_other[mirrored(m, bits)])] if m else [own[n]]
        return jnp.concatenate(pieces, axis=0)

    w_qkv_half = lax.dynamic_slice_in_dim(w_qkv, core * half, half, 0)
    dn, dn_other, partial = {0: w_down_half}, {}, {}
    wq, wq_other = {0: w_qkv_half}, {}
    for m in direct:
        dn[m] = row_step(dn[0], bits_of(m))
    gate_early, up_early = (dot(columns[0], weights(n, early)) for n in own)
    gate = gate_early + dot(columns[1], weights("gate", late))
    up_proj = up_early + dot(columns[1], weights("up", late))
    hidden = (gate / (1 + jnp.exp(-gate)) * up_proj).astype(bf16)
    partial[0] = dot(hidden, w_down).astype(bf16)
    turned = turned_halves(hidden)
    first_sent = partial[0]

    def down_product(m):
        return dot(turned, jnp.concatenate([dn[m], dn_other[mirrored(m, bits)]], axis=0)).astype(bf16)

    from_low = col % 2 == 1
    place_even = jnp.where(from_low, cols - 1 - col, col)
    place_odd = jnp.where(from_low, col, cols - 1 - col)
    by_even, by_odd = {}, {}

    def placed_at(t, place, places):
        value = None
        for c in places:
            if 0 <= t - c < rows:
                value = partial[t - c] if value is None else jnp.where(place == c, partial[t - c], value)
        return value

    def bases(t):
        return [placed_at(t, place_even, range(0, cols - 1, 2)), placed_at(t, place_odd, range(1, cols - 1, 2))]

    def terms(k):
        found = {}
        for c in range(cols):
            if c > 0:
                found.setdefault((c % 2, k + c - 1), []).append(c)
            if c < cols - 1:
                found.setdefault(((c + 1) % 2, k + cols - 2 - c), []).append(c)
        return found

    def summed(k):
        total = partial[k].astype(f32)
        for (is_even, t), where in terms(k).items():
            came = (by_even if is_even else by_odd)[t].astype(f32)
            counts = functools.reduce(jnp.logical_or, [col == c for c in where])
            total = total + jnp.where(counts, came, 0)
        return total

    next_gains = next_gain.reshape(rows, 1, block)
    squares, fresh, scaled = {}, {}, {}

    def finish(k):
        m = frames[k]
        fresh[k] = (blocks[m].astype(f32) + summed(k)).astype(bf16)
        v = fresh[k].astype(f32)
        squares[k] = jnp.sum(v * v, axis=-1, keepdims=True)
        out = (v * lax.dynamic_index_in_dim(next_gains, row_of(m), 0, False)).astype(bf16)
        scaled[k] = out if m == 0 else turned_halves(out)

    def terms_of(k):
        m = frames[k]
        low, high = scaled[k][:, :half], scaled[k][:, half:]
        if m == 0:
            return [(low, w_qkv, 0), (high, w_qkv, 1)]
        return [(low, wq[m], 0), (high, wq_other[mirrored(m, bits)], 0)]

    place_of = {m: k for k, m in enumerate(frames)}
    steps = rows + cols - 2
    ready = barrier(tuple(dn[m] for m in direct) + (first_sent,))
    for m, value in zip(direct, ready):
        dn[m] = value
        dn_other[m] = swap_cores(value)
    for mask, held, bit in order:
        if held:
            dn[mask] = row_step(dn[held], bit)
    acc, last_step = None, ()
    scalars = jnp.stack([(w_qkv.shape[1] // HD) * col, row_of(frames[-1]) == col]).astype(jnp.int32)

    def tie(store, masks, values):
        for m, value in zip(masks, values):
            store[m] = value

    for t in range(steps):
        base = bases(t)
        sends = []
        for i, came in enumerate((by_odd.get(t - 1), by_even.get(t - 1))):
            if base[i] is not None:
                send = base[i]
                if came is not None:
                    came = came.astype(f32)
                    send = send.astype(f32) + (jnp.where(at_end, 0, came) if i == 0 else came)
                sends.append((i, first_sent if t == 0 else send.astype(bf16)))
        held_now = {1: [(dn, relayed), (partial, [place_of[m] for m in direct])], 2: [(dn_other, relayed), (wq, direct[:1])],
                    3: [(wq, direct[1:]), (wq_other, direct[:1]), (partial, [place_of[m] for m in relayed])],
                    4: [(wq, relayed), (wq_other, direct[1:])]}.get(t, [])
        done = t - cols
        if done >= 0:
            held_now = held_now + [(fresh, [done]), (scaled, [done])]
        flat = [store[m] for store, masks in held_now for m in masks]
        extra = [acc] if t == steps - 1 else []
        ready = barrier(tuple(v for _, v in sends) + tuple(flat) + tuple(last_step) + tuple(extra))
        for (i, _), send in zip(sends, ready):
            (by_even, by_odd)[i][t] = lax.ppermute(send, line_axes[i], (even, odd)[i])
        at = len(sends)
        for store, masks in held_now:
            tie(store, masks, ready[at:at + len(masks)])
            at += len(masks)
        if extra:
            acc = ready[-1]
        if t > 0:
            for (i, _), value in zip(sent_before, ready[at:]):
                (by_even, by_odd)[i][t - 1] = value
        sent_before = sends
        last_step = [(by_even, by_odd)[i][t] for i, _ in sends]
        if t == 0:
            for m in direct:
                partial[place_of[m]] = barrier(down_product(m))
        elif t == 1:
            for m in relayed:
                dn_other[m] = swap_cores(dn[m])
            for m in direct[:1]:
                wq[m] = row_step(wq[0], bits_of(m))
        elif t == 2:
            for m in direct[1:]:
                wq[m] = row_step(wq[0], bits_of(m))
            for m in direct[:1]:
                wq_other[m] = swap_cores(wq[m])
            for m in relayed:
                partial[place_of[m]] = barrier(down_product(m))
        elif t == 3:
            for m in direct[1:]:
                wq_other[m] = swap_cores(wq[m])
            for mask, held, bit in order:
                if held:
                    wq[mask] = row_step(wq[held], bit)
        elif t == 4:
            for m in relayed:
                wq_other[m] = swap_cores(wq[m])
        k = t - (cols - 1)
        if k >= 0:
            finish(k)
        if k == rows - 3:
            acc = project(None, [x for j in range(rows - 2) for x in terms_of(j)], scalars)
    acc = project(acc, terms_of(rows - 2), scalars)
    finish(rows - 1)

    kept = fresh[0]
    for k in range(1, rows - 1):
        kept = jnp.where(row_of(frames[k]) == col, fresh[k], kept)
    moved_qkv, moved_residual = project(
        acc, terms_of(rows - 1), scalars,
        (sum(squares.values()), q_gain.reshape(1, HD), k_gain.reshape(1, HD), fresh[rows - 1], kept), d_model)
    return (moved_residual, moved_qkv)


def solution(mesh):
    return jax.shard_map(
        per_device,
        mesh=mesh,
        in_specs=(
            P(("rep", "row"), "col"),
            P(),
            P("row", "col"),
            P("row", "col"),
            P("col", "row"),
            P(),
            P("row", "col"),
            P(),
            P(),
            P(("rep", "row")),
        ),
        out_specs=(P(("rep", "row"), "col"), P(("rep", "row"), "col")),
        check_vma=False,
    )
```

```python
import functools

import jax
import jax.numpy as jnp
from jax import lax
from jax.experimental import pallas as pl
from jax.experimental.pallas import tpu as pltpu
from jax.sharding import PartitionSpec as P

HEADS = 16
KV_HEADS = 8
HD = 128
epsilon = 1e-06
bf16, f32 = jnp.bfloat16, jnp.float32
VMEM_LIMIT = 48 * 1024 * 1024


def swap_cores(x):
    return lax.ppermute(x, "rep", [(0, 1), (1, 0)])


def bits_of(n):
    return n.bit_length() - 1


def after(x, *done):
    return lax.optimization_barrier((x,) + done)[0] if done else x


def mirrored(mask, bits):
    return sum(1 << (bits - 1 - b) for b in range(bits) if mask >> b & 1)


def row_step(x, step):
    rows = lax.axis_size("row")
    last = bits_of(rows) - 1
    pairs = []
    for core in range(2):
        mask = 1 << (step if core == 0 else last - step)
        pairs += [(core * rows + i, core * rows + (i ^ mask)) for i in range(rows)]
    return lax.ppermute(x, ("rep", "row"), pairs)


def transfers(rows):
    order = [(1 << step, 0, step) for step in range(bits_of(rows))]
    for step in range(bits_of(rows)):
        order += [(held | 1 << step, held, step) for held in range(1, 1 << step)]
    return order


def tile_of(n):
    return next(t for t in (512, 256, 128, n) if n % t == 0)


def halves_kernel(core_ref, top_ref, bottom_ref, out_ref, sems):
    half = top_ref.shape[0] // 2
    rows = pl.ds(pl.multiple_of(core_ref[0] * half, half), half)
    first = pltpu.make_async_copy(top_ref.at[rows], out_ref.at[pl.ds(0, half)], sems.at[0])
    second = pltpu.make_async_copy(bottom_ref.at[rows], out_ref.at[pl.ds(half, half)], sems.at[1])
    first.start()
    second.start()
    first.wait()
    second.wait()


def core_halves(core, top, bottom):
    anywhere = pl.BlockSpec(memory_space=pl.ANY)
    return pl.pallas_call(
        halves_kernel,
        in_specs=[pl.BlockSpec(memory_space=pltpu.SMEM), anywhere, anywhere],
        out_specs=pl.BlockSpec(memory_space=pltpu.VMEM),
        out_shape=jax.ShapeDtypeStruct(top.shape, bf16),
        scratch_shapes=[pltpu.SemaphoreType.DMA((2,))],
        cost_estimate=pl.CostEstimate(flops=0, bytes_accessed=4 * top.size, transcendentals=0),
    )(core, top, bottom)


def project_kernel(n, has_acc, d_model, at_ref, *refs):
    lhs, ws, rest = refs[:n], refs[n:2 * n], refs[2 * n:]
    x = jnp.concatenate([r[...] for r in lhs], axis=1)
    w = jnp.concatenate([r[...] for r in ws], axis=0)
    v = jnp.dot(x, w, preferred_element_type=f32)
    if has_acc:
        v = v + rest[0][...]
    if d_model is None:
        rest[-1][...] = v
        return
    squares_ref, q_gain_ref, k_gain_ref, fresh_ref, other_ref, out_ref, moved_ref = rest[-7:]
    moved_ref[...] = jnp.where(at_ref[1] == 1, fresh_ref[...], other_ref[...])
    v = v * lax.rsqrt(squares_ref[...] / d_model + epsilon)
    heads = v.shape[1] // HD
    for h in range(heads):
        number = at_ref[0] + pl.program_id(0) * heads + h
        one = v[:, h * HD:(h + 1) * HD]
        gain = jnp.where(number < HEADS, q_gain_ref[...], k_gain_ref[...])
        normed = one * lax.rsqrt(jnp.mean(one * one, axis=-1, keepdims=True) + epsilon) * gain
        out_ref[:, h * HD:(h + 1) * HD] = jnp.where(number < HEADS + KV_HEADS, normed, one).astype(bf16)


def project(acc, terms, scalars, final=None, d_model=None):
    tok, depth = terms[0][0].shape
    width = terms[0][1].shape[1]
    tn = tile_of(width)
    n = len(terms)
    tile = pl.BlockSpec((tok, tn), lambda i: (0, i))
    in_specs = [pl.BlockSpec(memory_space=pltpu.SMEM)]
    in_specs += [pl.BlockSpec((tok, depth), lambda i: (0, 0))] * n
    in_specs += [pl.BlockSpec((depth, tn), functools.partial(lambda r, i: (r, i), r)) for _, _, r in terms]
    args = [t[0] for t in terms] + [t[1] for t in terms]
    if acc is not None:
        in_specs, args = in_specs + [tile], args + [acc]
    if final is not None:
        block = final[-1].shape[1]
        moved = pl.BlockSpec((tok, block // (width // tn)), lambda i: (0, i))
        in_specs += [pl.BlockSpec((tok, 1), lambda i: (0, 0))] + [pl.BlockSpec((1, HD), lambda i: (0, 0))] * 2
        in_specs += [moved] * 2
        args += list(final)
    out_specs, out_shape = tile, jax.ShapeDtypeStruct((tok, width), f32)
    if final is not None:
        out_specs = [tile, moved]
        out_shape = [jax.ShapeDtypeStruct((tok, width), bf16), jax.ShapeDtypeStruct((tok, block), bf16)]
    return pl.pallas_call(
        functools.partial(project_kernel, n, acc is not None, d_model),
        grid=(width // tn,),
        in_specs=in_specs,
        out_specs=out_specs,
        out_shape=out_shape,
        compiler_params=pltpu.CompilerParams(vmem_limit_bytes=VMEM_LIMIT),
        cost_estimate=pl.CostEstimate(flops=2 * n * tok * depth * width,
                                      bytes_accessed=2 * n * depth * (width + tok) + 8 * tok * width, transcendentals=0),
    )(scalars, *args)


def per_device(residual, post_gain, w_gate, w_up, w_down, next_gain, w_qkv, q_gain, k_gain, source):
    rows, cols = lax.axis_size("row"), lax.axis_size("col")
    me, core, col = lax.axis_index("row"), lax.axis_index("rep"), lax.axis_index("col")
    tok, width = residual.shape
    d_model = width * cols
    block = d_model // rows
    half = block // 2
    bits = bits_of(rows)
    order = transfers(rows)
    direct = [o[0] for o in order if o[1] == 0]
    relayed = [o[0] for o in order if o[1] != 0]
    frames = [0] + direct + relayed

    def row_of(mask):
        return me ^ jnp.where(core == 0, mask, mirrored(mask, bits))

    barrier = lax.optimization_barrier
    even = [(i, i ^ 1) for i in range(cols)]
    odd = [(cols * r + i, cols * r + (i - 1 ^ 1) + 1) for r in range(2) for i in range(1, cols - 1)]
    odd += [(cols * r + i, cols * (1 - r) + i) for r in range(2) for i in (0, cols - 1)]
    line_axes = ("col", ("rep", "col"))
    at_end = (col == 0) | (col == cols - 1)
    ff = w_gate.shape[1]
    ff_half = ff // 2
    last_mask = frames[-1]

    own = {"gate": w_gate, "up": w_up}
    gu = {0: core_halves(core.astype(jnp.int32).reshape(1), w_gate, w_up)}

    my_block = core * rows + me
    from_peer = after(source, gu[0]) // tok != my_block
    picked = source % tok + tok * from_peer.astype(jnp.int32)
    onehot = (picked[:, None] == jnp.arange(2 * tok, dtype=jnp.int32)[None, :]).astype(bf16)
    both = jnp.concatenate([residual, swap_cores(residual)], axis=0)
    placed = jnp.dot(onehot, both, preferred_element_type=f32).astype(bf16)

    by_even, by_odd = {0: placed}, {0: placed}
    left_over = cols - 1
    step = 0

    def line_step():
        nonlocal step
        if step < left_over:
            step += 1
            by_even[step] = lax.ppermute(by_odd[step - 1], "col", even)
            if step < left_over:
                by_odd[step] = lax.ppermute(by_even[step - 1], line_axes[1], odd)

    for m in direct:
        gu[m] = row_step(gu[0], bits_of(m))
    for _ in range(left_over):
        line_step()
    before = max(left_over - 1, 0)
    ready = barrier(tuple(gu[m] for m in direct) + (by_even[before], by_odd[before]))
    for m, value in zip(direct, ready):
        gu[m] = value
    by_even[before], by_odd[before] = ready[len(direct):]
    for mask, held, bit in order:
        if held:
            gu[mask] = row_step(gu[held], bit)

    arrived = [placed] + [by_even[t] for t in range(1, cols)] + [by_odd[t] for t in range(1, cols - 1)]
    place = [[0 if j == c else (abs(j - c) if (c % 2 == 1) == (j < c) else cols - 1 + abs(j - c))
              for j in range(cols)] for c in range(cols)]
    where_is = jnp.asarray(place, jnp.int32)[col]
    line = jnp.stack(arrived)
    blocks = {m: lax.dynamic_index_in_dim(line, where_is[row_of(m)], 0, False) for m in frames}

    squares = sum(jnp.sum(jnp.square(blocks[m].astype(f32)), axis=-1, keepdims=True) for m in frames)
    scale = lax.rsqrt(squares / d_model + epsilon)
    gains = post_gain.reshape(rows, block)

    def turned_halves(x):
        width = x.shape[1] // 2
        low, high = x[:, :width], x[:, width:]
        return jnp.concatenate([jnp.where(core == 0, low, high), jnp.where(core == 0, high, low)], axis=1)

    def normed(m):
        out = (blocks[m].astype(f32) * scale * lax.dynamic_index_in_dim(gains, row_of(m), 0, False)).astype(bf16)
        return out if m == 0 else turned_halves(out)

    def dot(x, w):
        return jnp.dot(x, w, preferred_element_type=f32)

    early, late = [0] + direct, relayed
    columns = [jnp.concatenate([normed(m) for m in ms], axis=1) for ms in (early, late)]

    w_down_half = lax.dynamic_slice_in_dim(w_down, core * ff_half, ff_half, 0)
    gu_other = {m: swap_cores(gu[m]) for m in direct}

    def weights(n, masks):
        pieces, at = [], half * (n == "up")
        for m in masks:
            pieces += [x[at:at + half] for x in (gu[m], gu_other[mirrored(m, bits)])] if m else [own[n]]
        return jnp.concatenate(pieces, axis=0)

    w_qkv_half = lax.dynamic_slice_in_dim(w_qkv, core * half, half, 0)
    gate_early, up_early = (dot(columns[0], weights(n, early)) for n in own)
    ready = barrier(tuple(gu[m] for m in relayed) + (gate_early, up_early, columns[1], w_down_half))
    for m, value in zip(relayed, ready):
        gu[m] = value
        gu_other[m] = swap_cores(value)
    gate_early, up_early, late_columns, w_down_half = ready[len(relayed):]
    columns = (columns[0], late_columns)
    dn, dn_other, partial = {0: w_down_half}, {}, {}
    wq, wq_other = {0: w_qkv_half}, {}
    for m in direct:
        dn[m] = row_step(dn[0], bits_of(m))
    gate = gate_early + dot(columns[1], weights("gate", late))
    up_proj = up_early + dot(columns[1], weights("up", late))
    hidden = (gate / (1 + jnp.exp(-gate)) * up_proj).astype(bf16)
    partial[0] = dot(hidden, w_down).astype(bf16)
    turned = turned_halves(hidden)
    first_sent = partial[0]

    def down_product(m):
        return dot(turned, jnp.concatenate([dn[m], dn_other[mirrored(m, bits)]], axis=0)).astype(bf16)

    from_low = col % 2 == 1
    place_even = jnp.where(from_low, cols - 1 - col, col)
    place_odd = jnp.where(from_low, col, cols - 1 - col)
    by_even, by_odd = {}, {}

    def placed_at(t, place, places):
        value = None
        for c in places:
            if 0 <= t - c < rows:
                value = partial[t - c] if value is None else jnp.where(place == c, partial[t - c], value)
        return value

    def bases(t):
        return [placed_at(t, place_even, range(0, cols - 1, 2)), placed_at(t, place_odd, range(1, cols - 1, 2))]

    def terms(k):
        found = {}
        for c in range(cols):
            if c > 0:
                found.setdefault((c % 2, k + c - 1), []).append(c)
            if c < cols - 1:
                found.setdefault(((c + 1) % 2, k + cols - 2 - c), []).append(c)
        return found

    def summed(k):
        total = partial[k].astype(f32)
        for (is_even, t), where in terms(k).items():
            came = (by_even if is_even else by_odd)[t].astype(f32)
            counts = functools.reduce(jnp.logical_or, [col == c for c in where])
            total = total + jnp.where(counts, came, 0)
        return total

    next_gains = next_gain.reshape(rows, 1, block)
    squares, fresh, scaled = {}, {}, {}

    def finish(k):
        m = frames[k]
        fresh[k] = (blocks[m].astype(f32) + summed(k)).astype(bf16)
        v = fresh[k].astype(f32)
        squares[k] = jnp.sum(v * v, axis=-1, keepdims=True)
        out = (v * lax.dynamic_index_in_dim(next_gains, row_of(m), 0, False)).astype(bf16)
        scaled[k] = out if m == 0 else turned_halves(out)

    def terms_of(k):
        m = frames[k]
        low, high = scaled[k][:, :half], scaled[k][:, half:]
        if m == 0:
            return [(low, w_qkv, 0), (high, w_qkv, 1)]
        return [(low, wq[m], 0), (high, wq_other[mirrored(m, bits)], 0)]

    place_of = {m: k for k, m in enumerate(frames)}
    steps = rows + cols - 2
    ready = barrier(tuple(dn[m] for m in direct) + (first_sent,))
    for m, value in zip(direct, ready):
        dn[m] = value
        dn_other[m] = swap_cores(value)
    for mask, held, bit in order:
        if held:
            dn[mask] = row_step(dn[held], bit)
    acc, last_step = None, ()
    scalars = jnp.stack([(w_qkv.shape[1] // HD) * col, row_of(frames[-1]) == col]).astype(jnp.int32)

    def tie(store, masks, values):
        for m, value in zip(masks, values):
            store[m] = value

    for t in range(steps):
        base = bases(t)
        sends = []
        for i, came in enumerate((by_odd.get(t - 1), by_even.get(t - 1))):
            if base[i] is not None:
                send = base[i]
                if came is not None:
                    came = came.astype(f32)
                    send = send.astype(f32) + (jnp.where(at_end, 0, came) if i == 0 else came)
                sends.append((i, first_sent if t == 0 else send.astype(bf16)))
        held_now = {1: [(partial, [place_of[m] for m in direct])], 2: [(dn_other, relayed), (wq, direct[:1])],
                    3: [(wq, direct[1:]), (wq_other, direct[:1]), (partial, [place_of[m] for m in relayed])],
                    4: [(wq, relayed), (wq_other, direct[1:])]}.get(t, [])
        done = t - cols
        if done >= 0:
            held_now = held_now + [(fresh, [done]), (scaled, [done])]
        flat = [store[m] for store, masks in held_now for m in masks]
        extra = [acc] if t == steps - 1 else []
        ready = barrier(tuple(v for _, v in sends) + tuple(flat) + tuple(last_step) + tuple(extra))
        for (i, _), send in zip(sends, ready):
            (by_even, by_odd)[i][t] = lax.ppermute(send, line_axes[i], (even, odd)[i])
        at = len(sends)
        for store, masks in held_now:
            tie(store, masks, ready[at:at + len(masks)])
            at += len(masks)
        if extra:
            acc = ready[-1]
        if t > 0:
            for (i, _), value in zip(sent_before, ready[at:]):
                (by_even, by_odd)[i][t - 1] = value
        sent_before = sends
        last_step = [(by_even, by_odd)[i][t] for i, _ in sends]
        if t == 0:
            for m in direct:
                partial[place_of[m]] = barrier(down_product(m))
        elif t == 1:
            for m in relayed:
                dn_other[m] = swap_cores(dn[m])
            for m in direct[:1]:
                wq[m] = row_step(wq[0], bits_of(m))
        elif t == 2:
            for m in direct[1:]:
                wq[m] = row_step(wq[0], bits_of(m))
            for m in direct[:1]:
                wq_other[m] = swap_cores(wq[m])
            for m in relayed:
                partial[place_of[m]] = barrier(down_product(m))
        elif t == 3:
            for m in direct[1:]:
                wq_other[m] = swap_cores(wq[m])
            for mask, held, bit in order:
                if held:
                    wq[mask] = row_step(wq[held], bit)
        elif t == 4:
            for m in relayed:
                wq_other[m] = swap_cores(wq[m])
        k = t - (cols - 1)
        if k >= 0:
            finish(k)
        if k == rows - 3:
            acc = project(None, [x for j in range(rows - 2) for x in terms_of(j)], scalars)
    acc = project(acc, terms_of(rows - 2), scalars)
    finish(rows - 1)

    kept = fresh[0]
    for k in range(1, rows - 1):
        kept = jnp.where(row_of(frames[k]) == col, fresh[k], kept)
    moved_qkv, moved_residual = project(
        acc, terms_of(rows - 1), scalars,
        (sum(squares.values()), q_gain.reshape(1, HD), k_gain.reshape(1, HD), fresh[rows - 1], kept), d_model)
    return (moved_residual, moved_qkv)


def solution(mesh):
    return jax.shard_map(
        per_device,
        mesh=mesh,
        in_specs=(
            P(("rep", "row"), "col"),
            P(),
            P("row", "col"),
            P("row", "col"),
            P("col", "row"),
            P(),
            P("row", "col"),
            P(),
            P(),
            P(("rep", "row")),
        ),
        out_specs=(P(("rep", "row"), "col"), P(("rep", "row"), "col")),
        check_vma=False,
    )
```

```python
import functools

import jax
import jax.numpy as jnp
from jax import lax
from jax.experimental import pallas as pl
from jax.experimental.pallas import tpu as pltpu
from jax.sharding import PartitionSpec as P

HEADS = 16
KV_HEADS = 8
HD = 128
epsilon = 1e-06
bf16, f32 = jnp.bfloat16, jnp.float32
VMEM_LIMIT = 48 * 1024 * 1024


def swap_cores(x):
    return lax.ppermute(x, "rep", [(0, 1), (1, 0)])


def bits_of(n):
    return n.bit_length() - 1


def after(x, *done):
    return lax.optimization_barrier((x,) + done)[0] if done else x


def mirrored(mask, bits):
    return sum(1 << (bits - 1 - b) for b in range(bits) if mask >> b & 1)


def row_step(x, step):
    rows = lax.axis_size("row")
    last = bits_of(rows) - 1
    pairs = []
    for core in range(2):
        mask = 1 << (step if core == 0 else last - step)
        pairs += [(core * rows + i, core * rows + (i ^ mask)) for i in range(rows)]
    return lax.ppermute(x, ("rep", "row"), pairs)


def transfers(rows):
    order = [(1 << step, 0, step) for step in range(bits_of(rows))]
    for step in range(bits_of(rows)):
        order += [(held | 1 << step, held, step) for held in range(1, 1 << step)]
    return order


def tile_of(n):
    return next(t for t in (512, 256, 128, n) if n % t == 0)


def halves_kernel(core_ref, top_ref, bottom_ref, out_ref, sems):
    half = top_ref.shape[0] // 2
    rows = pl.ds(pl.multiple_of(core_ref[0] * half, half), half)
    first = pltpu.make_async_copy(top_ref.at[rows], out_ref.at[pl.ds(0, half)], sems.at[0])
    second = pltpu.make_async_copy(bottom_ref.at[rows], out_ref.at[pl.ds(half, half)], sems.at[1])
    first.start()
    second.start()
    first.wait()
    second.wait()


def core_halves(core, top, bottom):
    anywhere = pl.BlockSpec(memory_space=pl.ANY)
    return pl.pallas_call(
        halves_kernel,
        in_specs=[pl.BlockSpec(memory_space=pltpu.SMEM), anywhere, anywhere],
        out_specs=pl.BlockSpec(memory_space=pltpu.VMEM),
        out_shape=jax.ShapeDtypeStruct(top.shape, bf16),
        scratch_shapes=[pltpu.SemaphoreType.DMA((2,))],
        cost_estimate=pl.CostEstimate(flops=0, bytes_accessed=4 * top.size, transcendentals=0),
    )(core, top, bottom)


def project_kernel(n, has_acc, d_model, at_ref, *refs):
    lhs, ws, rest = refs[:n], refs[n:2 * n], refs[2 * n:]
    x = jnp.concatenate([r[...] for r in lhs], axis=1)
    w = jnp.concatenate([r[...] for r in ws], axis=0)
    v = jnp.dot(x, w, preferred_element_type=f32)
    if has_acc:
        v = v + rest[0][...]
    if d_model is None:
        rest[-1][...] = v
        return
    squares_ref, q_gain_ref, k_gain_ref, fresh_ref, other_ref, out_ref, moved_ref = rest[-7:]
    moved_ref[...] = jnp.where(at_ref[1] == 1, fresh_ref[...], other_ref[...])
    v = v * lax.rsqrt(squares_ref[...] / d_model + epsilon)
    heads = v.shape[1] // HD
    for h in range(heads):
        number = at_ref[0] + pl.program_id(0) * heads + h
        one = v[:, h * HD:(h + 1) * HD]
        gain = jnp.where(number < HEADS, q_gain_ref[...], k_gain_ref[...])
        normed = one * lax.rsqrt(jnp.mean(one * one, axis=-1, keepdims=True) + epsilon) * gain
        out_ref[:, h * HD:(h + 1) * HD] = jnp.where(number < HEADS + KV_HEADS, normed, one).astype(bf16)


def project(acc, terms, scalars, final=None, d_model=None):
    tok, depth = terms[0][0].shape
    width = terms[0][1].shape[1]
    tn = tile_of(width)
    n = len(terms)
    tile = pl.BlockSpec((tok, tn), lambda i: (0, i))
    in_specs = [pl.BlockSpec(memory_space=pltpu.SMEM)]
    in_specs += [pl.BlockSpec((tok, depth), lambda i: (0, 0))] * n
    in_specs += [pl.BlockSpec((depth, tn), functools.partial(lambda r, i: (r, i), r)) for _, _, r in terms]
    args = [t[0] for t in terms] + [t[1] for t in terms]
    if acc is not None:
        in_specs, args = in_specs + [tile], args + [acc]
    if final is not None:
        block = final[-1].shape[1]
        moved = pl.BlockSpec((tok, block // (width // tn)), lambda i: (0, i))
        in_specs += [pl.BlockSpec((tok, 1), lambda i: (0, 0))] + [pl.BlockSpec((1, HD), lambda i: (0, 0))] * 2
        in_specs += [moved] * 2
        args += list(final)
    out_specs, out_shape = tile, jax.ShapeDtypeStruct((tok, width), f32)
    if final is not None:
        out_specs = [tile, moved]
        out_shape = [jax.ShapeDtypeStruct((tok, width), bf16), jax.ShapeDtypeStruct((tok, block), bf16)]
    return pl.pallas_call(
        functools.partial(project_kernel, n, acc is not None, d_model),
        grid=(width // tn,),
        in_specs=in_specs,
        out_specs=out_specs,
        out_shape=out_shape,
        compiler_params=pltpu.CompilerParams(vmem_limit_bytes=VMEM_LIMIT),
        cost_estimate=pl.CostEstimate(flops=2 * n * tok * depth * width,
                                      bytes_accessed=2 * n * depth * (width + tok) + 8 * tok * width, transcendentals=0),
    )(scalars, *args)


def per_device(residual, post_gain, w_gate, w_up, w_down, next_gain, w_qkv, q_gain, k_gain, source):
    rows, cols = lax.axis_size("row"), lax.axis_size("col")
    me, core, col = lax.axis_index("row"), lax.axis_index("rep"), lax.axis_index("col")
    tok, width = residual.shape
    d_model = width * cols
    block = d_model // rows
    half = block // 2
    bits = bits_of(rows)
    order = transfers(rows)
    direct = [o[0] for o in order if o[1] == 0]
    relayed = [o[0] for o in order if o[1] != 0]
    frames = [0] + direct + relayed

    def row_of(mask):
        return me ^ jnp.where(core == 0, mask, mirrored(mask, bits))

    barrier = lax.optimization_barrier
    even = [(i, i ^ 1) for i in range(cols)]
    odd = [(cols * r + i, cols * r + (i - 1 ^ 1) + 1) for r in range(2) for i in range(1, cols - 1)]
    odd += [(cols * r + i, cols * (1 - r) + i) for r in range(2) for i in (0, cols - 1)]
    line_axes = ("col", ("rep", "col"))
    at_end = (col == 0) | (col == cols - 1)
    ff = w_gate.shape[1]
    ff_half = ff // 2
    last_mask = frames[-1]

    own = {"gate": w_gate, "up": w_up}
    gu = {0: core_halves(core.astype(jnp.int32).reshape(1), w_gate, w_up)}

    my_block = core * rows + me
    from_peer = after(source, gu[0]) // tok != my_block
    picked = source % tok + tok * from_peer.astype(jnp.int32)
    onehot = (picked[:, None] == jnp.arange(2 * tok, dtype=jnp.int32)[None, :]).astype(bf16)
    both = jnp.concatenate([residual, swap_cores(residual)], axis=0)
    placed = jnp.dot(onehot, both, preferred_element_type=f32).astype(bf16)

    by_even, by_odd = {0: placed}, {0: placed}
    left_over = cols - 1
    step = 0

    def line_step():
        nonlocal step
        if step < left_over:
            step += 1
            by_even[step] = lax.ppermute(by_odd[step - 1], "col", even)
            if step < left_over:
                by_odd[step] = lax.ppermute(by_even[step - 1], line_axes[1], odd)

    for m in direct:
        gu[m] = row_step(gu[0], bits_of(m))
    for _ in range(left_over):
        line_step()
    before = max(left_over - 1, 0)
    ready = barrier(tuple(gu[m] for m in direct) + (by_even[before], by_odd[before]))
    for m, value in zip(direct, ready):
        gu[m] = value
    by_even[before], by_odd[before] = ready[len(direct):]
    for mask, held, bit in order:
        if held:
            gu[mask] = row_step(gu[held], bit)

    arrived = [placed] + [by_even[t] for t in range(1, cols)] + [by_odd[t] for t in range(1, cols - 1)]
    place = [[0 if j == c else (abs(j - c) if (c % 2 == 1) == (j < c) else cols - 1 + abs(j - c))
              for j in range(cols)] for c in range(cols)]
    where_is = jnp.asarray(place, jnp.int32)[col]
    line = jnp.stack(arrived)
    blocks = {m: lax.dynamic_index_in_dim(line, where_is[row_of(m)], 0, False) for m in frames}

    squares = sum(jnp.sum(jnp.square(blocks[m].astype(f32)), axis=-1, keepdims=True) for m in frames)
    scale = lax.rsqrt(squares / d_model + epsilon)
    gains = post_gain.reshape(rows, block)

    def turned_halves(x):
        width = x.shape[1] // 2
        low, high = x[:, :width], x[:, width:]
        return jnp.concatenate([jnp.where(core == 0, low, high), jnp.where(core == 0, high, low)], axis=1)

    def normed(m):
        out = (blocks[m].astype(f32) * scale * lax.dynamic_index_in_dim(gains, row_of(m), 0, False)).astype(bf16)
        return out if m == 0 else turned_halves(out)

    def dot(x, w):
        return jnp.dot(x, w, preferred_element_type=f32)

    early, late = [0] + direct, relayed
    columns = [jnp.concatenate([normed(m) for m in ms], axis=1) for ms in (early, late)]

    w_down_half = lax.dynamic_slice_in_dim(w_down, core * ff_half, ff_half, 0)
    gu_other = {m: swap_cores(gu[m]) for m in direct}

    def weights(n, masks):
        pieces, at = [], half * (n == "up")
        for m in masks:
            pieces += [x[at:at + half] for x in (gu[m], gu_other[mirrored(m, bits)])] if m else [own[n]]
        return jnp.concatenate(pieces, axis=0)

    w_qkv_half = lax.dynamic_slice_in_dim(w_qkv, core * half, half, 0)
    gate_early, up_early = (dot(columns[0], weights(n, early)) for n in own)
    ready = barrier(tuple(gu[m] for m in relayed) + (gate_early, up_early, columns[1], w_down_half))
    for m, value in zip(relayed, ready):
        gu[m] = value
        gu_other[m] = swap_cores(value)
    gate_early, up_early, late_columns, w_down_half = ready[len(relayed):]
    columns = (columns[0], late_columns)
    dn, dn_other, partial = {0: w_down_half}, {}, {}
    wq, wq_other = {0: w_qkv_half}, {}
    for m in direct:
        dn[m] = row_step(dn[0], bits_of(m))
    gate = gate_early + dot(columns[1], weights("gate", late))
    up_proj = up_early + dot(columns[1], weights("up", late))
    hidden = (gate / (1 + jnp.exp(-gate)) * up_proj).astype(bf16)
    partial[0] = dot(hidden, w_down).astype(bf16)
    turned = turned_halves(hidden)
    first_sent = partial[0]

    def down_product(m):
        return dot(turned, jnp.concatenate([dn[m], dn_other[mirrored(m, bits)]], axis=0)).astype(bf16)

    from_low = col % 2 == 1
    place_even = jnp.where(from_low, cols - 1 - col, col)
    place_odd = jnp.where(from_low, col, cols - 1 - col)
    by_even, by_odd = {}, {}

    def placed_at(t, place, places):
        value = None
        for c in places:
            if 0 <= t - c < rows:
                value = partial[t - c] if value is None else jnp.where(place == c, partial[t - c], value)
        return value

    def bases(t):
        return [placed_at(t, place_even, range(0, cols - 1, 2)), placed_at(t, place_odd, range(1, cols - 1, 2))]

    def terms(k):
        found = {}
        for c in range(cols):
            if c > 0:
                found.setdefault((c % 2, k + c - 1), []).append(c)
            if c < cols - 1:
                found.setdefault(((c + 1) % 2, k + cols - 2 - c), []).append(c)
        return found

    def summed(k):
        total = partial[k].astype(f32)
        for (is_even, t), where in terms(k).items():
            came = (by_even if is_even else by_odd)[t].astype(f32)
            counts = functools.reduce(jnp.logical_or, [col == c for c in where])
            total = total + jnp.where(counts, came, 0)
        return total

    next_gains = next_gain.reshape(rows, 1, block)
    squares, fresh, scaled = {}, {}, {}

    def finish(k):
        m = frames[k]
        fresh[k] = (blocks[m].astype(f32) + summed(k)).astype(bf16)
        v = fresh[k].astype(f32)
        squares[k] = jnp.sum(v * v, axis=-1, keepdims=True)
        out = (v * lax.dynamic_index_in_dim(next_gains, row_of(m), 0, False)).astype(bf16)
        scaled[k] = out if m == 0 else turned_halves(out)

    def terms_of(k):
        m = frames[k]
        low, high = scaled[k][:, :half], scaled[k][:, half:]
        if m == 0:
            return [(low, w_qkv, 0), (high, w_qkv, 1)]
        return [(low, wq[m], 0), (high, wq_other[mirrored(m, bits)], 0)]

    place_of = {m: k for k, m in enumerate(frames)}
    steps = rows + cols - 2
    ready = barrier(tuple(dn[m] for m in direct) + (first_sent,))
    for m, value in zip(direct, ready):
        dn[m] = value
        dn_other[m] = swap_cores(value)
    for mask, held, bit in order:
        if held:
            dn[mask] = row_step(dn[held], bit)
    acc, last_step = None, ()
    scalars = jnp.stack([(w_qkv.shape[1] // HD) * col, row_of(frames[-1]) == col]).astype(jnp.int32)

    def tie(store, masks, values):
        for m, value in zip(masks, values):
            store[m] = value

    for t in range(steps):
        base = bases(t)
        sends = []
        for i, came in enumerate((by_odd.get(t - 1), by_even.get(t - 1))):
            if base[i] is not None:
                send = base[i]
                if came is not None:
                    came = came.astype(f32)
                    send = send.astype(f32) + (jnp.where(at_end, 0, came) if i == 0 else came)
                sends.append((i, first_sent if t == 0 else send.astype(bf16)))
        held_now = {1: [(partial, [place_of[m] for m in direct])], 2: [(dn_other, relayed), (wq, direct[:1])],
                    3: [(wq, direct[1:]), (wq_other, direct[:1]), (partial, [place_of[m] for m in relayed])],
                    4: [(wq, relayed), (wq_other, direct[1:])]}.get(t, [])
        done = t - cols
        if done >= 0:
            held_now = held_now + [(fresh, [done]), (scaled, [done])]
        flat = [store[m] for store, masks in held_now for m in masks]
        extra = [acc] if t == steps - 1 else []
        ready = barrier(tuple(v for _, v in sends) + tuple(flat) + tuple(last_step) + tuple(extra))
        for (i, _), send in zip(sends, ready):
            (by_even, by_odd)[i][t] = lax.ppermute(send, line_axes[i], (even, odd)[i])
        at = len(sends)
        for store, masks in held_now:
            tie(store, masks, ready[at:at + len(masks)])
            at += len(masks)
        if extra:
            acc = ready[-1]
        if t > 0:
            for (i, _), value in zip(sent_before, ready[at:]):
                (by_even, by_odd)[i][t - 1] = value
        sent_before = sends
        last_step = [(by_even, by_odd)[i][t] for i, _ in sends]
        if t == 0:
            for m in direct:
                partial[place_of[m]] = barrier(down_product(m))
        elif t == 1:
            for m in relayed:
                dn_other[m] = swap_cores(dn[m])
            for m in direct[:1]:
                wq[m] = row_step(wq[0], bits_of(m))
        elif t == 2:
            for m in direct[1:]:
                wq[m] = row_step(wq[0], bits_of(m))
            for m in direct[:1]:
                wq_other[m] = swap_cores(wq[m])
            for m in relayed:
                partial[place_of[m]] = barrier(down_product(m))
        elif t == 3:
            for m in direct[1:]:
                wq_other[m] = swap_cores(wq[m])
            for mask, held, bit in order:
                if held:
                    wq[mask] = row_step(wq[held], bit)
        elif t == 4:
            for m in relayed:
                wq_other[m] = swap_cores(wq[m])
        k = t - (cols - 1)
        if k >= 0:
            finish(k)
        if k == rows - 3:
            acc = project(None, [x for j in range(rows - 3) for x in terms_of(j)], scalars)
    acc = project(acc, [x for j in (rows - 3, rows - 2) for x in terms_of(j)], scalars)
    finish(rows - 1)

    kept = fresh[0]
    for k in range(1, rows - 1):
        kept = jnp.where(row_of(frames[k]) == col, fresh[k], kept)
    moved_qkv, moved_residual = project(
        acc, terms_of(rows - 1), scalars,
        (sum(squares.values()), q_gain.reshape(1, HD), k_gain.reshape(1, HD), fresh[rows - 1], kept), d_model)
    return (moved_residual, moved_qkv)


def solution(mesh):
    return jax.shard_map(
        per_device,
        mesh=mesh,
        in_specs=(
            P(("rep", "row"), "col"),
            P(),
            P("row", "col"),
            P("row", "col"),
            P("col", "row"),
            P(),
            P("row", "col"),
            P(),
            P(),
            P(("rep", "row")),
        ),
        out_specs=(P(("rep", "row"), "col"), P(("rep", "row"), "col")),
        check_vma=False,
    )
```

```python
import functools

import jax
import jax.numpy as jnp
from jax import lax
from jax.experimental import pallas as pl
from jax.experimental.pallas import tpu as pltpu
from jax.sharding import PartitionSpec as P

HEADS = 16
KV_HEADS = 8
HD = 128
epsilon = 1e-06
bf16, f32 = jnp.bfloat16, jnp.float32
VMEM_LIMIT = 48 * 1024 * 1024


def swap_cores(x):
    return lax.ppermute(x, "rep", [(0, 1), (1, 0)])


def bits_of(n):
    return n.bit_length() - 1


def after(x, *done):
    return lax.optimization_barrier((x,) + done)[0] if done else x


def mirrored(mask, bits):
    return sum(1 << (bits - 1 - b) for b in range(bits) if mask >> b & 1)


def row_step(x, step):
    rows = lax.axis_size("row")
    last = bits_of(rows) - 1
    pairs = []
    for core in range(2):
        mask = 1 << (step if core == 0 else last - step)
        pairs += [(core * rows + i, core * rows + (i ^ mask)) for i in range(rows)]
    return lax.ppermute(x, ("rep", "row"), pairs)


def transfers(rows):
    order = [(1 << step, 0, step) for step in range(bits_of(rows))]
    for step in range(bits_of(rows)):
        order += [(held | 1 << step, held, step) for held in range(1, 1 << step)]
    return order


def tile_of(n):
    return next(t for t in (512, 256, 128, n) if n % t == 0)


def halves_kernel(core_ref, top_ref, bottom_ref, out_ref, sems):
    half = top_ref.shape[0] // 2
    rows = pl.ds(pl.multiple_of(core_ref[0] * half, half), half)
    first = pltpu.make_async_copy(top_ref.at[rows], out_ref.at[pl.ds(0, half)], sems.at[0])
    second = pltpu.make_async_copy(bottom_ref.at[rows], out_ref.at[pl.ds(half, half)], sems.at[1])
    first.start()
    second.start()
    first.wait()
    second.wait()


def core_halves(core, top, bottom):
    anywhere = pl.BlockSpec(memory_space=pl.ANY)
    return pl.pallas_call(
        halves_kernel,
        in_specs=[pl.BlockSpec(memory_space=pltpu.SMEM), anywhere, anywhere],
        out_specs=pl.BlockSpec(memory_space=pltpu.VMEM),
        out_shape=jax.ShapeDtypeStruct(top.shape, bf16),
        scratch_shapes=[pltpu.SemaphoreType.DMA((2,))],
        cost_estimate=pl.CostEstimate(flops=0, bytes_accessed=4 * top.size, transcendentals=0),
    )(core, top, bottom)


def project_kernel(n, has_acc, d_model, at_ref, *refs):
    lhs, ws, rest = refs[:n], refs[n:2 * n], refs[2 * n:]
    x = jnp.concatenate([r[...] for r in lhs], axis=1)
    w = jnp.concatenate([r[...] for r in ws], axis=0)
    v = jnp.dot(x, w, preferred_element_type=f32)
    if has_acc:
        v = v + rest[0][...]
    if d_model is None:
        rest[-1][...] = v
        return
    squares_ref, q_gain_ref, k_gain_ref, fresh_ref, other_ref, out_ref, moved_ref = rest[-7:]
    moved_ref[...] = jnp.where(at_ref[1] == 1, fresh_ref[...], other_ref[...])
    v = v * lax.rsqrt(squares_ref[...] / d_model + epsilon)
    heads = v.shape[1] // HD
    for h in range(heads):
        number = at_ref[0] + pl.program_id(0) * heads + h
        one = v[:, h * HD:(h + 1) * HD]
        gain = jnp.where(number < HEADS, q_gain_ref[...], k_gain_ref[...])
        normed = one * lax.rsqrt(jnp.mean(one * one, axis=-1, keepdims=True) + epsilon) * gain
        out_ref[:, h * HD:(h + 1) * HD] = jnp.where(number < HEADS + KV_HEADS, normed, one).astype(bf16)


def project(acc, terms, scalars, final=None, d_model=None):
    tok, depth = terms[0][0].shape
    width = terms[0][1].shape[1]
    tn = tile_of(width)
    n = len(terms)
    tile = pl.BlockSpec((tok, tn), lambda i: (0, i))
    in_specs = [pl.BlockSpec(memory_space=pltpu.SMEM)]
    in_specs += [pl.BlockSpec((tok, depth), lambda i: (0, 0))] * n
    in_specs += [pl.BlockSpec((depth, tn), functools.partial(lambda r, i: (r, i), r)) for _, _, r in terms]
    args = [t[0] for t in terms] + [t[1] for t in terms]
    if acc is not None:
        in_specs, args = in_specs + [tile], args + [acc]
    if final is not None:
        block = final[-1].shape[1]
        moved = pl.BlockSpec((tok, block // (width // tn)), lambda i: (0, i))
        in_specs += [pl.BlockSpec((tok, 1), lambda i: (0, 0))] + [pl.BlockSpec((1, HD), lambda i: (0, 0))] * 2
        in_specs += [moved] * 2
        args += list(final)
    out_specs, out_shape = tile, jax.ShapeDtypeStruct((tok, width), f32)
    if final is not None:
        out_specs = [tile, moved]
        out_shape = [jax.ShapeDtypeStruct((tok, width), bf16), jax.ShapeDtypeStruct((tok, block), bf16)]
    return pl.pallas_call(
        functools.partial(project_kernel, n, acc is not None, d_model),
        grid=(width // tn,),
        in_specs=in_specs,
        out_specs=out_specs,
        out_shape=out_shape,
        compiler_params=pltpu.CompilerParams(vmem_limit_bytes=VMEM_LIMIT),
        cost_estimate=pl.CostEstimate(flops=2 * n * tok * depth * width,
                                      bytes_accessed=2 * n * depth * (width + tok) + 8 * tok * width, transcendentals=0),
    )(scalars, *args)


def per_device(residual, post_gain, w_gate, w_up, w_down, next_gain, w_qkv, q_gain, k_gain, source):
    rows, cols = lax.axis_size("row"), lax.axis_size("col")
    me, core, col = lax.axis_index("row"), lax.axis_index("rep"), lax.axis_index("col")
    tok, width = residual.shape
    d_model = width * cols
    block = d_model // rows
    half = block // 2
    bits = bits_of(rows)
    order = transfers(rows)
    direct = [o[0] for o in order if o[1] == 0]
    relayed = [o[0] for o in order if o[1] != 0]
    frames = [0] + direct + relayed

    def row_of(mask):
        return me ^ jnp.where(core == 0, mask, mirrored(mask, bits))

    barrier = lax.optimization_barrier
    even = [(i, i ^ 1) for i in range(cols)]
    odd = [(cols * r + i, cols * r + (i - 1 ^ 1) + 1) for r in range(2) for i in range(1, cols - 1)]
    odd += [(cols * r + i, cols * (1 - r) + i) for r in range(2) for i in (0, cols - 1)]
    line_axes = ("col", ("rep", "col"))
    at_end = (col == 0) | (col == cols - 1)
    ff = w_gate.shape[1]
    ff_half = ff // 2
    last_mask = frames[-1]

    own = {"gate": w_gate, "up": w_up}
    gu = {0: core_halves(core.astype(jnp.int32).reshape(1), w_gate, w_up)}

    my_block = core * rows + me
    from_peer = after(source, gu[0]) // tok != my_block
    picked = source % tok + tok * from_peer.astype(jnp.int32)
    onehot = (picked[:, None] == jnp.arange(2 * tok, dtype=jnp.int32)[None, :]).astype(bf16)
    both = jnp.concatenate([residual, swap_cores(residual)], axis=0)
    placed = jnp.dot(onehot, both, preferred_element_type=f32).astype(bf16)

    by_even, by_odd = {0: placed}, {0: placed}
    left_over = cols - 1
    step = 0

    def line_step():
        nonlocal step
        if step < left_over:
            step += 1
            by_even[step] = lax.ppermute(by_odd[step - 1], "col", even)
            if step < left_over:
                by_odd[step] = lax.ppermute(by_even[step - 1], line_axes[1], odd)

    for m in direct:
        gu[m] = row_step(gu[0], bits_of(m))
    for _ in range(left_over):
        line_step()
    before = max(left_over - 1, 0)
    ready = barrier(tuple(gu[m] for m in direct) + (by_even[before], by_odd[before]))
    for m, value in zip(direct, ready):
        gu[m] = value
    by_even[before], by_odd[before] = ready[len(direct):]
    for mask, held, bit in order:
        if held:
            gu[mask] = row_step(gu[held], bit)

    arrived = [placed] + [by_even[t] for t in range(1, cols)] + [by_odd[t] for t in range(1, cols - 1)]
    place = [[0 if j == c else (abs(j - c) if (c % 2 == 1) == (j < c) else cols - 1 + abs(j - c))
              for j in range(cols)] for c in range(cols)]
    where_is = jnp.asarray(place, jnp.int32)[col]
    line = jnp.stack(arrived)
    blocks = {m: lax.dynamic_index_in_dim(line, where_is[row_of(m)], 0, False) for m in frames}

    squares = sum(jnp.sum(jnp.square(blocks[m].astype(f32)), axis=-1, keepdims=True) for m in frames)
    scale = lax.rsqrt(squares / d_model + epsilon)
    gains = post_gain.reshape(rows, block)

    def turned_halves(x):
        width = x.shape[1] // 2
        low, high = x[:, :width], x[:, width:]
        return jnp.concatenate([jnp.where(core == 0, low, high), jnp.where(core == 0, high, low)], axis=1)

    def normed(m):
        out = (blocks[m].astype(f32) * scale * lax.dynamic_index_in_dim(gains, row_of(m), 0, False)).astype(bf16)
        return out if m == 0 else turned_halves(out)

    def dot(x, w):
        return jnp.dot(x, w, preferred_element_type=f32)

    early, late = [0] + direct, relayed
    columns = [jnp.concatenate([normed(m) for m in ms], axis=1) for ms in (early, late)]

    w_down_half = lax.dynamic_slice_in_dim(w_down, core * ff_half, ff_half, 0)
    gu_other = {m: swap_cores(gu[m]) for m in direct}

    def weights(n, masks):
        pieces, at = [], half * (n == "up")
        for m in masks:
            pieces += [x[at:at + half] for x in (gu[m], gu_other[mirrored(m, bits)])] if m else [own[n]]
        return jnp.concatenate(pieces, axis=0)

    w_qkv_half = lax.dynamic_slice_in_dim(w_qkv, core * half, half, 0)
    gate_early, up_early = (dot(columns[0], weights(n, early)) for n in own)
    ready = barrier(tuple(gu[m] for m in relayed) + (gate_early, up_early, columns[1], w_down_half))
    for m, value in zip(relayed, ready):
        gu[m] = value
        gu_other[m] = swap_cores(value)
    gate_early, up_early, late_columns, w_down_half = ready[len(relayed):]
    columns = (columns[0], late_columns)
    dn, dn_other, partial = {0: w_down_half}, {}, {}
    wq, wq_other = {0: w_qkv_half}, {}
    for m in direct:
        dn[m] = row_step(dn[0], bits_of(m))
    gate = gate_early + dot(columns[1], weights("gate", late))
    up_proj = up_early + dot(columns[1], weights("up", late))
    hidden = (gate / (1 + jnp.exp(-gate)) * up_proj).astype(bf16)
    partial[0] = dot(hidden, w_down).astype(bf16)
    turned = turned_halves(hidden)
    first_sent = partial[0]

    def down_product(m):
        return dot(turned, jnp.concatenate([dn[m], dn_other[mirrored(m, bits)]], axis=0)).astype(bf16)

    from_low = col % 2 == 1
    place_even = jnp.where(from_low, cols - 1 - col, col)
    place_odd = jnp.where(from_low, col, cols - 1 - col)
    by_even, by_odd = {}, {}

    def placed_at(t, place, places):
        value = None
        for c in places:
            if 0 <= t - c < rows:
                value = partial[t - c] if value is None else jnp.where(place == c, partial[t - c], value)
        return value

    def bases(t):
        return [placed_at(t, place_even, range(0, cols - 1, 2)), placed_at(t, place_odd, range(1, cols - 1, 2))]

    def terms(k):
        found = {}
        for c in range(cols):
            if c > 0:
                found.setdefault((c % 2, k + c - 1), []).append(c)
            if c < cols - 1:
                found.setdefault(((c + 1) % 2, k + cols - 2 - c), []).append(c)
        return found

    def summed(k):
        total = partial[k].astype(f32)
        for (is_even, t), where in terms(k).items():
            came = (by_even if is_even else by_odd)[t].astype(f32)
            counts = functools.reduce(jnp.logical_or, [col == c for c in where])
            total = total + jnp.where(counts, came, 0)
        return total

    next_gains = next_gain.reshape(rows, 1, block)
    squares, fresh, scaled = {}, {}, {}

    def finish(k):
        m = frames[k]
        fresh[k] = (blocks[m].astype(f32) + summed(k)).astype(bf16)
        v = fresh[k].astype(f32)
        squares[k] = jnp.sum(v * v, axis=-1, keepdims=True)
        out = (v * lax.dynamic_index_in_dim(next_gains, row_of(m), 0, False)).astype(bf16)
        scaled[k] = out if m == 0 else turned_halves(out)

    def terms_of(k):
        m = frames[k]
        low, high = scaled[k][:, :half], scaled[k][:, half:]
        if m == 0:
            return [(low, w_qkv, 0), (high, w_qkv, 1)]
        return [(low, wq[m], 0), (high, wq_other[mirrored(m, bits)], 0)]

    place_of = {m: k for k, m in enumerate(frames)}
    steps = rows + cols - 2
    ready = barrier(tuple(dn[m] for m in direct) + (first_sent,))
    for m, value in zip(direct, ready):
        dn[m] = value
        dn_other[m] = swap_cores(value)
    for mask, held, bit in order:
        if held:
            dn[mask] = row_step(dn[held], bit)
    acc, last_step = None, ()
    scalars = jnp.stack([(w_qkv.shape[1] // HD) * col, row_of(frames[-1]) == col]).astype(jnp.int32)

    def tie(store, masks, values):
        for m, value in zip(masks, values):
            store[m] = value

    for t in range(steps):
        base = bases(t)
        sends = []
        for i, came in enumerate((by_odd.get(t - 1), by_even.get(t - 1))):
            if base[i] is not None:
                send = base[i]
                if came is not None:
                    came = came.astype(f32)
                    send = send.astype(f32) + (jnp.where(at_end, 0, came) if i == 0 else came)
                sends.append((i, first_sent if t == 0 else send.astype(bf16)))
        held_now = {1: [(partial, [place_of[m] for m in direct])], 2: [(dn_other, relayed), (wq, direct[:1])],
                    3: [(wq, direct[1:]), (wq_other, direct[:1]), (partial, [place_of[m] for m in relayed])],
                    4: [(wq, relayed), (wq_other, direct[1:])]}.get(t, [])
        done = t - cols
        if done >= 0:
            held_now = held_now + [(fresh, [done]), (scaled, [done])]
        flat = [store[m] for store, masks in held_now for m in masks]
        extra = [acc] if t == steps - 1 else []
        ready = barrier(tuple(v for _, v in sends) + tuple(flat) + tuple(last_step) + tuple(extra))
        for (i, _), send in reversed(list(zip(sends, ready))):
            (by_even, by_odd)[i][t] = lax.ppermute(send, line_axes[i], (even, odd)[i])
        at = len(sends)
        for store, masks in held_now:
            tie(store, masks, ready[at:at + len(masks)])
            at += len(masks)
        if extra:
            acc = ready[-1]
        if t > 0:
            for (i, _), value in zip(sent_before, ready[at:]):
                (by_even, by_odd)[i][t - 1] = value
        sent_before = sends
        last_step = [(by_even, by_odd)[i][t] for i, _ in sends]
        if t == 0:
            for m in direct:
                partial[place_of[m]] = barrier(down_product(m))
        elif t == 1:
            for m in relayed:
                dn_other[m] = swap_cores(dn[m])
            for m in direct[:1]:
                wq[m] = row_step(wq[0], bits_of(m))
        elif t == 2:
            for m in direct[1:]:
                wq[m] = row_step(wq[0], bits_of(m))
            for m in direct[:1]:
                wq_other[m] = swap_cores(wq[m])
            for m in relayed:
                partial[place_of[m]] = barrier(down_product(m))
        elif t == 3:
            for m in direct[1:]:
                wq_other[m] = swap_cores(wq[m])
            for mask, held, bit in order:
                if held:
                    wq[mask] = row_step(wq[held], bit)
        elif t == 4:
            for m in relayed:
                wq_other[m] = swap_cores(wq[m])
        k = t - (cols - 1)
        if k >= 0:
            finish(k)
        if k == rows - 3:
            acc = project(None, [x for j in range(rows - 3) for x in terms_of(j)], scalars)
    acc = project(acc, [x for j in (rows - 3, rows - 2) for x in terms_of(j)], scalars)
    finish(rows - 1)

    kept = fresh[0]
    for k in range(1, rows - 1):
        kept = jnp.where(row_of(frames[k]) == col, fresh[k], kept)
    moved_qkv, moved_residual = project(
        acc, terms_of(rows - 1), scalars,
        (sum(squares.values()), q_gain.reshape(1, HD), k_gain.reshape(1, HD), fresh[rows - 1], kept), d_model)
    return (moved_residual, moved_qkv)


def solution(mesh):
    return jax.shard_map(
        per_device,
        mesh=mesh,
        in_specs=(
            P(("rep", "row"), "col"),
            P(),
            P("row", "col"),
            P("row", "col"),
            P("col", "row"),
            P(),
            P("row", "col"),
            P(),
            P(),
            P(("rep", "row")),
        ),
        out_specs=(P(("rep", "row"), "col"), P(("rep", "row"), "col")),
        check_vma=False,
    )
```
